256 devices in a mesh: ctx: 32 (over z, x_lo, core), tp: 8 (over x_hi, y).
Axes of the slice: x: 4 (x_hi: 2, x_lo: 2; x = x_hi * 2 + x_lo), y: 4, z: 8, core: 2. Of those that a mesh axis runs over, the one named last changes fastest.
Arguments:
- tokens: bfloat16 [16384, 4608], P('ctx'), may hold values from -6 to 6
- norm_gain: float32 [4608], replicated, may hold values from 0.1 to 1.9
- q_weight: bfloat16 [4608, 2048], P(None, 'tp'), may hold values from -0.09375 to 0.09375
- k_weight: bfloat16 [4608, 1024], P(None, 'tp'), may hold values from -0.09375 to 0.09375
- v_weight: bfloat16 [4608, 1024], P(None, 'tp'), may hold values from -0.09375 to 0.09375
- o_weight: bfloat16 [2048, 4608], P('tp'), may hold values from -5.634757 to 5.634757
- post_gain: float32 [4608], P('tp'), may hold values from 0.1 to 1.9
- doc_ids: int32 [128], replicated, may hold values from 0 to 31, never falling along the last dimension, each value on 1 to 32 neighbouring positions
- plan: int32 [128], replicated, may hold values from 0 to 31, as said below
Outputs:
- attended: bfloat16 [16384, 4608], P('ctx', 'tp')
The draws below stay inside these ranges and needn't reach their ends.
Inputs may be any that keep to these rules, and one draw needn't show every extreme that they name: `plan`: every one of the 32 shards is named by exactly 4 blocks, and never by two of the 4 blocks that one index of ctx holds.
All inputs are finite; a program needn't handle non-finite values.
Results may differ from the reference program's by a relative error of at most 0.019.
Values may be sent and summed in bfloat16 or wider, within the bound.
No kernel may reach another device: no remote copies, remote signals or barrier semaphores. Data moves between devices by JAX's collectives and lax.ppermute only.
A program may use at most 128 MiB of HBM per device.

```python
import math
import jax
import jax.numpy as jnp
import numpy as np
from jax import lax

D = 4608
HEADS = 16
KV_HEADS = 8
HD = 128
BLK = 128
BLK_DEV = 4
NB = 128
TOKENS = 16384
DOCS = 32
MOST_DOC = 32
N_CTX = 32
N_TP = 8


def draw_o_weight(key, part):
    key = jax.random.fold_in(key, 11)
    entry_key, spread_key = jax.random.split(key)
    fan_rows = HEADS * HD
    column = jnp.arange(D, dtype=jnp.float32) / D
    factor = jax.random.uniform(spread_key, (D,), jnp.float32, 0.5, 1.5)
    entries = jnp.clip(jax.random.normal(entry_key, (fan_rows, D), jnp.float32), -4.0, 4.0)
    col_scale = 10.0 ** column
    return (entries * (col_scale * factor)[None, :] * fan_rows ** (-0.5)).astype(jnp.bfloat16)


def draw_plan(key, part):
    key = jax.random.fold_in(key, 23)
    first_key, second_key, third_key = jax.random.split(key, 3)
    outer_perm = jax.random.permutation(first_key, N_CTX)
    inner_perm = jax.random.permutation(second_key, N_CTX)
    shift_values = jax.random.permutation(third_key, N_CTX)[:BLK_DEV]
    block_ids = jnp.arange(NB, dtype=jnp.int32)
    source = block_ids // BLK_DEV
    return outer_perm[(inner_perm[source] + shift_values[block_ids % BLK_DEV]) % N_CTX].astype(jnp.int32)


def level_of(key, shape, pieces, smallest, top_value):
    factor_of = 1.0
    for axis_at, parts in pieces:
        heights = jax.random.uniform(jax.random.fold_in(jax.random.fold_in(key, 6), axis_at), (parts,), jnp.float32, smallest / len(pieces), top_value / len(pieces))
        factor_of = factor_of * jnp.repeat(jnp.exp(heights), shape[axis_at] // parts).reshape((-1,) + (1,) * (len(shape) - 1 - axis_at))
    return factor_of


def split_up(number_of, total, reach, skew):
    loads = [(1 << 20) // math.isqrt(rank ** skew) + 1 for rank in range(2, number_of + 1)]
    surplus, counts = total - reach - (number_of - 1), [1] * (number_of - 1)
    while surplus > 0:
        movable = [i for i in range(number_of - 1) if counts[i] < reach]
        pool, remaining = sum([loads[i] for i in movable]), surplus
        for i in movable:
            more = min(reach - counts[i], max(1, remaining * loads[i] // pool), surplus)
            counts[i] = counts[i] + more
            surplus = surplus - more
    return np.array([reach] + counts)


def uneven_parts(own_key, count, total, reach, slope):
    if count == 2:
        one = jax.random.randint(own_key, (), max(1, total - reach), min(reach, total - 1) + 1)
        return jnp.stack([one, total - one])
    sizes = jnp.asarray(split_up(count, total, reach, slope), jnp.int32)
    couples = (count - 1) // 2
    donor, taker = sizes[1:1 + 2 * couples:2], sizes[2:2 + 2 * couples:2]
    slack = jnp.minimum(donor - 1, reach - taker)
    shifted = jax.random.randint(jax.random.fold_in(own_key, 1), (couples,), 0, 1 << 20) % (slack + 1)
    sizes = sizes.at[1:1 + 2 * couples:2].set(donor - shifted).at[2:2 + 2 * couples:2].set(taker + shifted)
    return sizes[jax.random.permutation(jax.random.fold_in(own_key, 2), count)]


def centred(rng, extent, scale, bound, cuts=(), kind=jnp.bfloat16):
    level = level_of(rng, extent, cuts, -0.22, 0.18) if cuts else 1.0
    array = jax.random.normal(rng, extent, jnp.float32) * scale * level
    return jnp.minimum(jnp.maximum(array, -bound), bound).astype(kind)


def setup_inputs(seed: int = 0) -> dict:
    streams_of = jax.random.split(jax.random.key(seed), 10)
    tokens = centred(streams_of[0], (TOKENS, D), 1.0, 6.0, ((0, 32),))
    norm_gain = jnp.clip(1.0 + 0.18 * jax.random.normal(streams_of[1], (D,), jnp.float32), 0.1, 1.9)
    q_weight = centred(streams_of[2], (D, HEADS * HD), D ** -0.5, 0.09375, ((1, 8),))
    k_weight = centred(streams_of[3], (D, KV_HEADS * HD), D ** -0.5, 0.09375, ((1, 8),))
    v_weight = centred(streams_of[4], (D, KV_HEADS * HD), D ** -0.5, 0.09375, ((1, 8),))
    o_weight = draw_o_weight(jax.random.fold_in(streams_of[9], 71), 0)
    post_gain = jnp.clip(1.0 + 0.18 * jax.random.normal(streams_of[6], (D,), jnp.float32), 0.1, 1.9)
    doc_ids = jnp.searchsorted(jnp.cumsum(uneven_parts(streams_of[7], DOCS, NB, MOST_DOC, 2)), jnp.arange(NB), side="right").astype(jnp.int32)
    plan = draw_plan(jax.random.fold_in(streams_of[9], 71), 0)
    return {"tokens": tokens, "norm_gain": norm_gain, "q_weight": q_weight, "k_weight": k_weight, "v_weight": v_weight, "o_weight": o_weight, "post_gain": post_gain, "doc_ids": doc_ids, "plan": plan}


query_scale = 144.0 ** (-0.5)
soft_cap = 50.0
norm_eps = 1e-06

def reference(tokens, norm_gain, q_weight, k_weight, v_weight, o_weight, post_gain, doc_ids, plan):
    floated = tokens.astype(jnp.float32)
    normed = (floated * lax.rsqrt(lax.optimization_barrier(jnp.mean(floated * floated, axis=1, keepdims=True)) + norm_eps) * norm_gain).astype(jnp.bfloat16)
    queries = (jnp.dot(normed, q_weight, preferred_element_type=jnp.float32) * query_scale).astype(jnp.bfloat16)
    key_rows = jnp.dot(normed, k_weight, preferred_element_type=jnp.float32).astype(jnp.bfloat16)
    value_rows = jnp.dot(normed, v_weight, preferred_element_type=jnp.float32).astype(jnp.bfloat16)
    group_size = HEADS // KV_HEADS
    window = MOST_DOC * BLK
    pad_keys = jnp.concatenate([jnp.zeros((window, KV_HEADS * HD), jnp.bfloat16), key_rows], axis=0)
    pad_values = jnp.concatenate([jnp.zeros((window, KV_HEADS * HD), jnp.bfloat16), value_rows], axis=0)
    pad_docs = jnp.concatenate([jnp.full((MOST_DOC,), -1, jnp.int32), doc_ids.astype(jnp.int32)])
    offsets = jnp.arange(BLK, dtype=jnp.int32)

    def one_block(block_index):
        query_rows = lax.dynamic_slice_in_dim(queries, block_index * BLK, BLK, 0).astype(jnp.float32).reshape(BLK, KV_HEADS, group_size, HD)
        key_tile = lax.dynamic_slice_in_dim(pad_keys, (block_index + 1) * BLK, window, 0).astype(jnp.float32).reshape(window, KV_HEADS, HD)
        value_tile = lax.dynamic_slice_in_dim(pad_values, (block_index + 1) * BLK, window, 0).astype(jnp.float32).reshape(window, KV_HEADS, HD)
        key_docs = jnp.repeat(lax.dynamic_slice_in_dim(pad_docs, block_index + 1, MOST_DOC, 0), BLK)
        query_doc = lax.dynamic_index_in_dim(doc_ids.astype(jnp.int32), block_index, 0, keepdims=False)
        query_pos = block_index * BLK + offsets
        key_pos = (block_index + 1 - MOST_DOC) * BLK + jnp.arange(window, dtype=jnp.int32)
        allowed = (key_docs[None, :] == query_doc) & (key_pos[None, :] <= query_pos[:, None])
        scores = jnp.einsum('rngd,knd->ngrk', query_rows, key_tile)
        capped = soft_cap * jnp.tanh(scores / soft_cap)
        weights = jnp.where(allowed[None, None], jnp.exp(capped), 0.0)
        denominator = lax.optimization_barrier(jnp.sum(weights, axis=-1))
        rounded = lax.optimization_barrier(weights.astype(jnp.bfloat16)).astype(jnp.float32)
        weighted = jnp.einsum('ngrk,knd->rngd', rounded, value_tile)
        outcome = weighted / jnp.transpose(denominator, (2, 0, 1))[..., None]
        return outcome.reshape(BLK, HEADS * HD).astype(jnp.bfloat16)
    heads_out = lax.map(one_block, jnp.arange(NB, dtype=jnp.int32)).reshape(TOKENS, HEADS * HD)
    per_group = HEADS * HD // N_TP
    summed = jnp.zeros((TOKENS, D), jnp.float32)
    for group_index in range(N_TP):
        lower = group_index * per_group
        partial_value = jnp.dot(heads_out[:, lower:lower + per_group], o_weight[lower:lower + per_group], preferred_element_type=jnp.float32).astype(jnp.bfloat16)
        partial_value = lax.optimization_barrier(partial_value)
        summed = summed + partial_value.astype(jnp.float32)
    squares = lax.optimization_barrier(jnp.sum(summed * summed, axis=1, keepdims=True))
    normed_rows = (summed * lax.rsqrt(squares / D + norm_eps) * post_gain).astype(jnp.bfloat16)
    row_order = jnp.argsort(plan.astype(jnp.int32) * NB + jnp.arange(NB, dtype=jnp.int32))
    return normed_rows.reshape(NB, BLK, D)[row_order].reshape(TOKENS, D)
```

```python
import functools
import math

import jax
import jax.numpy as jnp
from jax import lax
from jax.experimental import pallas as pl
from jax.experimental.pallas import tpu as pltpu
from jax.sharding import PartitionSpec as P

HD = 128
BLK = 128
PLANE = 4
BACK = 2

query_scale = 144.0 ** (-0.5)
soft_cap = 50.0
norm_eps = 1e-06
LOG2E = math.log2(math.e)


def qkv_kernel(x_ref, g_ref, wq_ref, wk_ref, wv_ref, q_ref, kv_ref):
    x = x_ref[...].astype(jnp.float32)
    r = lax.rsqrt(jnp.mean(x * x, axis=1, keepdims=True) + norm_eps)
    normed = (x * r * g_ref[...]).astype(jnp.bfloat16)
    kv_ref[:, :HD] = jnp.dot(
        normed, wk_ref[...], preferred_element_type=jnp.float32
    ).astype(jnp.bfloat16)
    kv_ref[:, HD:] = jnp.dot(
        normed, wv_ref[...], preferred_element_type=jnp.float32
    ).astype(jnp.bfloat16)
    q_ref[...] = (
        jnp.dot(normed, wq_ref[...], preferred_element_type=jnp.float32) * query_scale
    ).astype(jnp.bfloat16)


def project(tokens, gain, wq, wk, wv):
    rows, d = tokens.shape
    tile = 128

    def whole(a):
        return pl.BlockSpec(a.shape, lambda i: (0, 0), pipeline_mode=pl.Buffered(1))

    return pl.pallas_call(
        qkv_kernel,
        grid=(rows // tile,),
        in_specs=[
            pl.BlockSpec((tile, d), lambda i: (i, 0)),
            whole(gain),
            whole(wq),
            whole(wk),
            whole(wv),
        ],
        out_specs=[
            pl.BlockSpec((tile, wq.shape[1]), lambda i: (i, 0)),
            pl.BlockSpec((tile, 2 * HD), lambda i: (i, 0)),
        ],
        out_shape=[
            jax.ShapeDtypeStruct((rows, wq.shape[1]), jnp.bfloat16),
            jax.ShapeDtypeStruct((rows, 2 * HD), jnp.bfloat16),
        ],
        compiler_params=pltpu.CompilerParams(vmem_limit_bytes=40 * 2**20),
        cost_estimate=pl.CostEstimate(
            flops=2 * rows * d * 4 * HD, bytes_accessed=2 * d * (rows + 4 * HD), transcendentals=0
        ),
        name="project",
    )(tokens, gain, wq, wk, wv)


def attend_kernel(parts, rows, info_ref, q_ref, *refs):
    kv_refs, out_ref, held, sems = refs[:parts], refs[parts], refs[parts + 1], refs[parts + 2]
    place = info_ref[0]
    copies = []
    for i in range(parts):
        slot = (i // PLANE) * PLANE + (place ^ (i % PLANE))
        copies.append(pltpu.make_async_copy(kv_refs[i], held.at[slot], sems.at[i]))
    for copy in copies:
        copy.start()
    for copy in copies:
        copy.wait()
    blocks = rows // BLK
    last = place + BACK * PLANE
    heads = q_ref.shape[1] // HD
    for b in range(blocks):
        span = slice(b * BLK, (b + 1) * BLK)
        q = jnp.concatenate([q_ref[span, h * HD : (h + 1) * HD] for h in range(heads)], axis=0)
        start = info_ref[1 + b]
        query_at = (
            last * rows + b * BLK + lax.broadcasted_iota(jnp.int32, (heads * BLK, rows), 0) % BLK
        )
        offset = lax.broadcasted_iota(jnp.int32, (heads * BLK, rows), 1)

        def step(s, carry):
            total, weight_sum = carry
            scores = lax.dot_general(
                q, held[s, :, :HD], (((1,), (1,)), ((), ())), preferred_element_type=jnp.float32
            )
            key_at = s * rows + offset
            allowed = (key_at >= start) & (key_at <= query_at)
            capped = jnp.tanh(scores * (1.0 / soft_cap)) * (soft_cap * LOG2E)
            weights = jnp.where(allowed, jnp.exp2(capped), 0.0)
            for j in range(rows // HD):
                weight_sum = weight_sum + weights[:, j * HD : (j + 1) * HD]
            total = total + jnp.dot(
                weights.astype(jnp.bfloat16), held[s, :, HD:], preferred_element_type=jnp.float32
            )
            return total, weight_sum

        zero = jnp.zeros((heads * BLK, HD), jnp.float32)
        total, weight_sum = lax.fori_loop(start // rows, last + 1, step, (zero, zero))
        done = (total / jnp.sum(weight_sum, axis=1, keepdims=True)).astype(jnp.bfloat16)
        for h in range(heads):
            out_ref[span, h * HD : (h + 1) * HD] = done[h * BLK : (h + 1) * BLK]


def attend(info, q, kvs):
    rows = q.shape[0]
    parts = len(kvs)
    return pl.pallas_call(
        functools.partial(attend_kernel, parts, rows),
        grid_spec=pltpu.PrefetchScalarGridSpec(
            num_scalar_prefetch=1,
            grid=(1,),
            in_specs=[pl.BlockSpec(q.shape, lambda i, s: (0, 0))]
            + [pl.BlockSpec(memory_space=pl.ANY)] * parts,
            out_specs=pl.BlockSpec(q.shape, lambda i, s: (0, 0)),
            scratch_shapes=[
                pltpu.VMEM((parts, rows, 2 * HD), jnp.bfloat16),
                pltpu.SemaphoreType.DMA((parts,)),
            ],
        ),
        out_shape=jax.ShapeDtypeStruct(q.shape, jnp.bfloat16),
        compiler_params=pltpu.CompilerParams(vmem_limit_bytes=32 * 2**20),
        cost_estimate=pl.CostEstimate(
            flops=2 * 10**9, bytes_accessed=4 * 10**6, transcendentals=8 * 10**6
        ),
        name="attend",
    )(info, q, *kvs)


def out_kernel(parts, *refs):
    total = jnp.dot(refs[0][...], refs[parts][...], preferred_element_type=jnp.float32)
    for i in range(1, parts):
        total = total + jnp.dot(
            refs[i][...], refs[parts + i][...], preferred_element_type=jnp.float32
        )
    refs[2 * parts][...] = total
    refs[2 * parts + 1][...] = jnp.sum(total * total, axis=1, keepdims=True)


def out_project(heads, weights):
    rows, inner = heads[0].shape
    cols = weights[0].shape[1]
    parts = len(heads)
    tile = 256
    return pl.pallas_call(
        functools.partial(out_kernel, parts),
        grid=(rows // tile,),
        in_specs=[pl.BlockSpec((tile, inner), lambda i: (i, 0))] * parts
        + [pl.BlockSpec((inner, cols), lambda i: (0, 0), pipeline_mode=pl.Buffered(1))] * parts,
        out_specs=[
            pl.BlockSpec((tile, cols), lambda i: (i, 0)),
            pl.BlockSpec((tile, 1), lambda i: (i, 0)),
        ],
        out_shape=[
            jax.ShapeDtypeStruct((rows, cols), jnp.float32),
            jax.ShapeDtypeStruct((rows, 1), jnp.float32),
        ],
        compiler_params=pltpu.CompilerParams(vmem_limit_bytes=32 * 2**20),
        cost_estimate=pl.CostEstimate(
            flops=2 * rows * inner * parts * cols, bytes_accessed=6 * 10**6, transcendentals=0
        ),
        name="out_project",
    )(*heads, *weights)


def local(n_ctx, n_tp, tokens, norm_gain, q_weight, k_weight, v_weight, o_weight, post_gain, doc_ids, plan):
    rows, features = tokens.shape
    blocks = rows // BLK
    total_blocks = doc_ids.shape[0]
    shard = lax.axis_index("ctx")
    group = lax.axis_index("tp")
    planes = n_ctx // PLANE
    cols = o_weight.shape[1] // n_tp

    def ctx_xor(a, m):
        return lax.ppermute(a, "ctx", [(i, i ^ m) for i in range(n_ctx)])

    def ctx_z(a, d):
        return lax.ppermute(a, "ctx", [(i, (i + d * PLANE) % n_ctx) for i in range(n_ctx)])

    def tp_xor(a, m):
        return lax.ppermute(a, "tp", [(i, i ^ m) for i in range(n_tp)])

    out_weights = [
        lax.dynamic_slice_in_dim(o_weight, (group ^ m) * cols, cols, axis=1) for m in range(n_tp)
    ]
    out_weights = [w if m == 0 else tp_xor(w, m) for m, w in enumerate(out_weights)]

    queries, own_kv = project(tokens, norm_gain.reshape(1, -1), q_weight, k_weight, v_weight)

    kvs = []
    for back in range(BACK, -1, -1):
        near = own_kv if back == 0 else ctx_z(own_kv, back)
        across = ctx_xor(near, 2)
        kvs += [near, ctx_xor(near, 1), across, ctx_xor(across, 1)]

    first_block = jnp.sum(
        (doc_ids[None, :] < doc_ids[:, None]).astype(jnp.int32), axis=1
    )
    own_first = lax.dynamic_slice_in_dim(first_block, shard * blocks, blocks, 0)
    plane_first = (shard // PLANE - BACK) * PLANE * blocks
    info = jnp.concatenate(
        [(shard % PLANE).reshape(1), (own_first - plane_first) * BLK]
    ).astype(jnp.int32)
    natural = attend(info, queries, kvs)

    width = natural.shape[1]
    piece = BLK // n_ctx
    same = (plan[None, :] == plan[:, None]).astype(jnp.int32)
    block_ids = jnp.arange(total_blocks, dtype=jnp.int32)
    rank = jnp.sum(same * (block_ids[None, :] < block_ids[:, None]), axis=1)
    target = plan * blocks + rank
    picker = (target[None, :] == block_ids[:, None]).astype(jnp.bfloat16)
    striped = natural.reshape(blocks, n_ctx, piece, width).transpose(1, 0, 2, 3)
    striped = striped.reshape(n_ctx, blocks, piece * width)
    gathered = lax.all_to_all(striped, "ctx", 0, 0, tiled=True)
    ordered = jnp.dot(
        picker,
        gathered.reshape(total_blocks, piece * width),
        preferred_element_type=jnp.float32,
    ).astype(jnp.bfloat16)
    placed = lax.all_to_all(
        ordered.reshape(n_ctx, blocks, piece * width), "ctx", 0, 0, tiled=True
    )
    placed = (
        placed.reshape(n_ctx, blocks, piece, width).transpose(1, 0, 2, 3).reshape(rows, width)
    )

    heads = [placed if m == 0 else tp_xor(placed, m) for m in range(n_tp)]
    summed, squares = out_project(heads, out_weights)
    squares = squares.reshape(rows)
    m = 1
    while m < n_tp:
        squares = squares + tp_xor(squares, m)
        m *= 2
    scale = lax.rsqrt(squares / features + norm_eps)
    return (summed * scale[:, None] * post_gain).astype(jnp.bfloat16)


def solution(mesh):
    placed = (
        P("ctx", None),
        P(),
        P(None, "tp"),
        P(None, "tp"),
        P(None, "tp"),
        P("tp", None),
        P("tp"),
        P(),
        P(),
    )
    return jax.shard_map(
        functools.partial(local, mesh.shape["ctx"], mesh.shape["tp"]),
        mesh=mesh,
        in_specs=placed,
        out_specs=P("ctx", "tp"),
        check_vma=False,
    )
```

```python
import functools
import math

import jax
import jax.numpy as jnp
from jax import lax
from jax.experimental import pallas as pl
from jax.experimental.pallas import tpu as pltpu
from jax.sharding import PartitionSpec as P

HD = 128
BLK = 128
PLANE = 4
BACK = 2

query_scale = 144.0 ** (-0.5)
soft_cap = 50.0
norm_eps = 1e-06
LOG2E = math.log2(math.e)


def project_kernel(scale, tile, count, x_hbm, g_ref, *refs):
    w_hbms, out_ref, x_buf, w_buf, x_sems, w_sems = (
        refs[:count],
        refs[count],
        refs[count + 1],
        refs[count + 2],
        refs[count + 3],
        refs[count + 4],
    )
    tiles = x_buf.shape[0]

    def x_copy(i):
        return pltpu.make_async_copy(
            x_hbm.at[pl.ds(pl.multiple_of(i * tile, tile), tile)], x_buf.at[i], x_sems.at[i]
        )

    width = w_buf.shape[1] // count
    w_copies = [
        pltpu.make_async_copy(
            w_hbms[j], w_buf.at[:, j * width : (j + 1) * width], w_sems.at[j]
        )
        for j in range(count)
    ]
    x_copy(0).start()
    for copy in w_copies:
        copy.start()
    for i in range(1, tiles):
        x_copy(i).start()

    @pl.loop(0, tiles)
    def _(i):
        x_copy(i).wait()
        x = x_buf[i].astype(jnp.float32)
        r = lax.rsqrt(jnp.mean(x * x, axis=1, keepdims=True) + norm_eps)
        normed = (x * r * g_ref[...]).astype(jnp.bfloat16)

        @pl.when(i == 0)
        def _():
            for copy in w_copies:
                copy.wait()

        done = jnp.dot(normed, w_buf[...], preferred_element_type=jnp.float32)
        if scale is not None:
            done = done * scale
        out_ref[pl.ds(pl.multiple_of(i * tile, tile), tile), :] = done.astype(jnp.bfloat16)


def project(tokens, gain, weights, scale, name, vmem):
    rows, d = tokens.shape
    tile = 128
    count = len(weights)
    width = sum(w.shape[1] for w in weights)
    return pl.pallas_call(
        functools.partial(project_kernel, scale, tile, count),
        in_specs=[pl.BlockSpec(memory_space=pl.ANY), pl.BlockSpec(memory_space=pltpu.VMEM)]
        + [pl.BlockSpec(memory_space=pl.ANY)] * count,
        out_specs=pl.BlockSpec(memory_space=pltpu.VMEM),
        out_shape=jax.ShapeDtypeStruct((rows, width), jnp.bfloat16),
        scratch_shapes=[
            pltpu.VMEM((rows // tile, tile, d), jnp.bfloat16),
            pltpu.VMEM((d, width), jnp.bfloat16),
            pltpu.SemaphoreType.DMA((rows // tile,)),
            pltpu.SemaphoreType.DMA((count,)),
        ],
        compiler_params=pltpu.CompilerParams(vmem_limit_bytes=vmem * 2**20),
        cost_estimate=pl.CostEstimate(
            flops=2 * rows * d * width, bytes_accessed=2 * d * (rows + width), transcendentals=0
        ),
        name=name,
    )(tokens, gain, *weights)


def attend_kernel(rows, stage, info_ref, q_ref, *refs):
    kv_refs, refs = refs[:PLANE], refs[PLANE:]
    if stage == 0:
        num_ref, den_ref, held, sems = refs
    elif stage < BACK:
        num_in, den_in, num_ref, den_ref, held, sems = refs
    else:
        num_in, den_in, out_ref, num_ref, den_ref, held, sems = refs
    place = info_ref[0]
    copies = [
        pltpu.make_async_copy(kv_refs[i], held.at[place ^ i], sems.at[i]) for i in range(PLANE)
    ]
    for copy in copies:
        copy.start()
    if stage == 0:
        num_ref[...] = jnp.zeros_like(num_ref)
        den_ref[...] = jnp.zeros_like(den_ref)
    else:
        num_ref[...] = num_in[...]
        den_ref[...] = den_in[...]
    blocks = rows // BLK
    heads = num_ref.shape[0]
    base = (BACK - stage) * PLANE
    starts = [info_ref[1 + b] - base * rows for b in range(blocks)]
    row = lax.broadcasted_iota(jnp.int32, (rows, 1), 0)
    start_row = jnp.full((rows, 1), starts[0], jnp.int32)
    for b in range(1, blocks):
        start_row = jnp.where(row >= b * BLK, starts[b], start_row)

    def tile(s, lower, causal):
        for h in range(heads):
            scores = lax.dot_general(
                q_ref[:, h * HD : (h + 1) * HD],
                held[s, :, :HD],
                (((1,), (1,)), ((), ())),
                preferred_element_type=jnp.float32,
            )
            capped = jnp.tanh(scores * (1.0 / soft_cap)) * (soft_cap * LOG2E)
            weights = jnp.exp2(capped)
            if lower or causal:
                offset = lax.broadcasted_iota(jnp.int32, (rows, rows), 1)
                allowed = offset >= start_row - s * rows
                if causal:
                    allowed = allowed & (offset <= row)
                weights = jnp.where(allowed, weights, 0.0)
            weight_sum = weights[:, :HD]
            for j in range(1, rows // HD):
                weight_sum = weight_sum + weights[:, j * HD : (j + 1) * HD]
            den_ref[h] += weight_sum
            num_ref[h] += jnp.dot(
                weights.astype(jnp.bfloat16), held[s, :, HD:], preferred_element_type=jnp.float32
            )

    end = place if stage == 0 else PLANE
    lo = jnp.clip(lax.div(jnp.maximum(starts[0], 0), rows), 0, end)
    clear = jnp.clip(lax.div(jnp.maximum(starts[-1], 0) + rows - 1, rows), lo, end)
    for copy in copies:
        copy.wait()

    @pl.loop(lo, clear)
    def _(s):
        tile(s, True, False)

    @pl.loop(clear, end)
    def _(s):
        tile(s, False, False)

    if stage == 0:
        tile(place, True, True)
    if stage == BACK:
        for h in range(heads):
            total = jnp.sum(den_ref[h], axis=1, keepdims=True)
            out_ref[:, h * HD : (h + 1) * HD] = (num_ref[h] / total).astype(jnp.bfloat16)


def attend(stage, info, q, kvs, carry):
    rows = q.shape[0]
    heads = q.shape[1] // HD
    sums = jax.ShapeDtypeStruct((heads, rows, HD), jnp.float32)
    last = stage == BACK
    whole = pl.BlockSpec(memory_space=pltpu.VMEM)
    return pl.pallas_call(
        functools.partial(attend_kernel, rows, stage),
        in_specs=[pl.BlockSpec(memory_space=pltpu.SMEM), whole]
        + [pl.BlockSpec(memory_space=pl.ANY)] * PLANE
        + [whole] * len(carry),
        out_specs=whole if last else [whole] * 2,
        out_shape=jax.ShapeDtypeStruct(q.shape, jnp.bfloat16) if last else [sums] * 2,
        scratch_shapes=([pltpu.VMEM(sums.shape, jnp.float32)] * 2 if last else [])
        + [
            pltpu.VMEM((PLANE, rows, 2 * HD), jnp.bfloat16),
            pltpu.SemaphoreType.DMA((PLANE,)),
        ],
        compiler_params=pltpu.CompilerParams(vmem_limit_bytes=32 * 2**20),
        cost_estimate=pl.CostEstimate(
            flops=2 * 10**9, bytes_accessed=4 * 10**6, transcendentals=4 * 10**6
        ),
        name="attend",
    )(info, q, *kvs, *carry)


def out_kernel(parts, *refs):
    w_ref, sum_ref, square_ref = refs[parts:]
    total = jnp.dot(refs[0][...], w_ref[0], preferred_element_type=jnp.float32)
    for i in range(1, parts):
        total = total + jnp.dot(refs[i][...], w_ref[i], preferred_element_type=jnp.float32)
    sum_ref[...] = total
    square_ref[...] = jnp.sum(total * total, axis=1, keepdims=True)


def out_project(heads, weights):
    rows, inner = heads[0].shape
    parts, _, cols = weights.shape
    tile = 256
    return pl.pallas_call(
        functools.partial(out_kernel, parts),
        grid=(rows // tile,),
        in_specs=[pl.BlockSpec((tile, inner), lambda i: (i, 0))] * parts
        + [pl.BlockSpec(weights.shape, lambda i: (0, 0, 0), pipeline_mode=pl.Buffered(1))],
        out_specs=[
            pl.BlockSpec((tile, cols), lambda i: (i, 0)),
            pl.BlockSpec((tile, 1), lambda i: (i, 0)),
        ],
        out_shape=[
            jax.ShapeDtypeStruct((rows, cols), jnp.float32),
            jax.ShapeDtypeStruct((rows, 1), jnp.float32),
        ],
        compiler_params=pltpu.CompilerParams(vmem_limit_bytes=32 * 2**20),
        cost_estimate=pl.CostEstimate(
            flops=2 * rows * inner * parts * cols, bytes_accessed=6 * 10**6, transcendentals=0
        ),
        name="out_project",
    )(*heads, weights)


def local(n_ctx, n_tp, tokens, norm_gain, q_weight, k_weight, v_weight, o_weight, post_gain, doc_ids, plan):
    rows, features = tokens.shape
    blocks = rows // BLK
    total_blocks = doc_ids.shape[0]
    shard = lax.axis_index("ctx")
    group = lax.axis_index("tp")
    cols = o_weight.shape[1] // n_tp
    inner = o_weight.shape[0]
    half = inner // 2
    core = shard % 2

    def ctx_xor(a, m):
        return lax.ppermute(a, "ctx", [(i, i ^ m) for i in range(n_ctx)])

    def ctx_z(a, d):
        return lax.ppermute(a, "ctx", [(i, (i + d * PLANE) % n_ctx) for i in range(n_ctx)])

    def tp_xor(a, m):
        return lax.ppermute(a, "tp", [(i, i ^ m) for i in range(n_tp)])

    gain = norm_gain.reshape(1, -1)
    own_kv = project(tokens, gain, [k_weight, v_weight], None, "project_kv", 56)

    own_weight = lax.dynamic_slice_in_dim(o_weight, group * cols, cols, axis=1)
    slices = [
        lax.dynamic_slice(o_weight, (core * half, (group ^ m) * cols), (half, cols))
        for m in range(1, n_tp)
    ]
    own_kv, slices = lax.optimization_barrier((own_kv, slices))

    kvs = []
    near = own_kv
    for back in range(BACK + 1):
        near = near if back == 0 else ctx_z(near, 1)
        across = ctx_xor(near, 2)
        kvs.append([near, ctx_xor(near, 1), across, ctx_xor(across, 1)])
    mine = jnp.stack([tp_xor(w, m + 1) for m, w in enumerate(slices)])
    theirs = ctx_xor(mine, 1)
    even = core == 0
    out_weights = jnp.concatenate(
        [jnp.where(even, mine, theirs), jnp.where(even, theirs, mine)], axis=1
    )
    out_weights = jnp.concatenate([own_weight[None], out_weights], axis=0)

    queries = project(tokens, gain, [q_weight], query_scale, "project_q", 40)

    first_block = jnp.sum((doc_ids[None, :] < doc_ids[:, None]).astype(jnp.int32), axis=1)
    own_first = lax.dynamic_slice_in_dim(first_block, shard * blocks, blocks, 0)
    plane_first = (shard // PLANE - BACK) * PLANE * blocks
    info = jnp.concatenate(
        [(shard % PLANE).reshape(1), (own_first - plane_first) * BLK]
    ).astype(jnp.int32)

    same = (plan[None, :] == plan[:, None]).astype(jnp.int32)
    block_ids = jnp.arange(total_blocks, dtype=jnp.int32)
    rank = jnp.sum(same * (block_ids[None, :] < block_ids[:, None]), axis=1)
    target = plan * blocks + rank
    picker = (target[None, :] == block_ids[:, None]).astype(jnp.bfloat16)

    carry = []
    for stage in range(BACK):
        carry = attend(stage, info, queries, kvs[stage], carry)
    carry, out_weights, picker = lax.optimization_barrier((carry, out_weights, picker))
    natural = attend(BACK, info, queries, kvs[BACK], carry)

    width = natural.shape[1]
    piece = BLK // n_ctx
    striped = natural.reshape(blocks, n_ctx, piece, width).transpose(1, 0, 2, 3)
    striped = striped.reshape(n_ctx, blocks, piece * width)
    gathered = lax.all_to_all(striped, "ctx", 0, 0, tiled=True)
    ordered = jnp.dot(
        picker,
        gathered.reshape(total_blocks, piece * width),
        preferred_element_type=jnp.float32,
    ).astype(jnp.bfloat16)
    placed = lax.all_to_all(
        ordered.reshape(n_ctx, blocks, piece * width), "ctx", 0, 0, tiled=True
    )
    placed = (
        placed.reshape(n_ctx, blocks, piece, width).transpose(1, 0, 2, 3).reshape(rows, width)
    )

    heads = [placed] + [None] * (n_tp - 1)
    for m in (4, 1, 3, 2):
        heads[m] = tp_xor(placed, m)
    heads[5] = tp_xor(heads[4], 1)
    heads[7] = tp_xor(heads[4], 3)
    heads[6] = tp_xor(heads[2], 4)
    summed, squares = out_project(heads, out_weights)
    squares = squares.reshape(rows)
    squares = squares + tp_xor(squares, 4)
    squares = squares + tp_xor(squares, 1) + tp_xor(squares, 3) + tp_xor(squares, 2)
    scale = lax.rsqrt(squares / features + norm_eps)
    return (summed * scale[:, None] * post_gain).astype(jnp.bfloat16)


def solution(mesh):
    placed = (
        P("ctx", None),
        P(),
        P(None, "tp"),
        P(None, "tp"),
        P(None, "tp"),
        P("tp", None),
        P("tp"),
        P(),
        P(),
    )
    return jax.shard_map(
        functools.partial(local, mesh.shape["ctx"], mesh.shape["tp"]),
        mesh=mesh,
        in_specs=placed,
        out_specs=P("ctx", "tp"),
        check_vma=False,
    )
```

```python
import functools
import math

import jax
import jax.numpy as jnp
from jax import lax
from jax.experimental import pallas as pl
from jax.experimental.pallas import tpu as pltpu
from jax.sharding import PartitionSpec as P

HD = 128
BLK = 128
PLANE = 4
BACK = 2

query_scale = 144.0 ** (-0.5)
soft_cap = 50.0
norm_eps = 1e-06
LOG2E = math.log2(math.e)


def project_kernel(scale, tile, count, x_hbm, g_ref, *refs):
    w_hbms, refs = refs[:count], refs[count:]
    out_ref, x_buf, normed_buf, w_buf, x_sems, w_sems = refs
    tiles = x_buf.shape[0] // tile

    def span(i):
        return pl.ds(pl.multiple_of(i * tile, tile), tile)

    def x_copy(i):
        return pltpu.make_async_copy(x_hbm.at[span(i)], x_buf.at[span(i)], x_sems.at[i])

    width = w_buf.shape[1] // count
    w_copies = [
        pltpu.make_async_copy(
            w_hbms[j], w_buf.at[:, j * width : (j + 1) * width], w_sems.at[j]
        )
        for j in range(count)
    ]
    for i in range(tiles):
        x_copy(i).start()
    for copy in w_copies:
        copy.start()
    gain = g_ref[...].reshape(1, -1)

    @pl.loop(0, tiles)
    def _(i):
        x_copy(i).wait()
        x = x_buf[span(i)].astype(jnp.float32)
        r = lax.rsqrt(jnp.mean(x * x, axis=1, keepdims=True) + norm_eps)
        normed_buf[span(i)] = (x * r * gain).astype(jnp.bfloat16)

    for copy in w_copies:
        copy.wait()
    done = jnp.dot(normed_buf[...], w_buf[...], preferred_element_type=jnp.float32)
    if scale is not None:
        done = done * scale
    out_ref[...] = done.astype(jnp.bfloat16)


def project(tokens, gain, weights, scale, name, vmem):
    rows, d = tokens.shape
    tile = 64
    count = len(weights)
    width = sum(w.shape[1] for w in weights)
    return pl.pallas_call(
        functools.partial(project_kernel, scale, tile, count),
        in_specs=[pl.BlockSpec(memory_space=pl.ANY), pl.BlockSpec(memory_space=pltpu.VMEM)]
        + [pl.BlockSpec(memory_space=pl.ANY)] * count,
        out_specs=pl.BlockSpec(memory_space=pltpu.VMEM),
        out_shape=jax.ShapeDtypeStruct((rows, width), jnp.bfloat16),
        scratch_shapes=[
            pltpu.VMEM((rows, d), jnp.bfloat16),
            pltpu.VMEM((rows, d), jnp.bfloat16),
            pltpu.VMEM((d, width), jnp.bfloat16),
            pltpu.SemaphoreType.DMA((rows // tile,)),
            pltpu.SemaphoreType.DMA((count,)),
        ],
        compiler_params=pltpu.CompilerParams(vmem_limit_bytes=vmem * 2**20),
        cost_estimate=pl.CostEstimate(
            flops=2 * rows * d * width, bytes_accessed=2 * d * (rows + width), transcendentals=0
        ),
        name=name,
    )(tokens, gain, *weights)


def attend_kernel(rows, stage, info_ref, q_ref, *refs):
    kv_refs, refs = refs[:PLANE], refs[PLANE:]
    if stage == 0:
        num_ref, den_ref, held, sems = refs
    elif stage < BACK:
        num_in, den_in, num_ref, den_ref, held, sems = refs
    else:
        num_in, den_in, out_ref, num_ref, den_ref, held, sems = refs
    place = info_ref[0]
    copies = [
        pltpu.make_async_copy(kv_refs[i], held.at[place ^ i], sems.at[i]) for i in range(PLANE)
    ]
    for copy in copies:
        copy.start()
    if stage == 0:
        num_ref[...] = jnp.zeros_like(num_ref)
        den_ref[...] = jnp.zeros_like(den_ref)
    else:
        num_ref[...] = num_in[...]
        den_ref[...] = den_in[...]
    blocks = rows // BLK
    heads = num_ref.shape[0]
    base = (BACK - stage) * PLANE
    starts = [info_ref[1 + b] - base * rows for b in range(blocks)]
    row = lax.broadcasted_iota(jnp.int32, (rows, 1), 0)
    start_row = jnp.full((rows, 1), starts[0], jnp.int32)
    for b in range(1, blocks):
        start_row = jnp.where(row >= b * BLK, starts[b], start_row)

    def tile(s, lower, causal):
        for h in range(heads):
            scores = lax.dot_general(
                q_ref[:, h * HD : (h + 1) * HD],
                held[s, :, :HD],
                (((1,), (1,)), ((), ())),
                preferred_element_type=jnp.float32,
            )
            capped = jnp.tanh(scores * (1.0 / soft_cap)) * (soft_cap * LOG2E)
            weights = jnp.exp2(capped)
            if lower or causal:
                offset = lax.broadcasted_iota(jnp.int32, (rows, rows), 1)
                allowed = offset >= start_row - s * rows
                if causal:
                    allowed = allowed & (offset <= row)
                weights = jnp.where(allowed, weights, 0.0)
            weight_sum = weights[:, :HD]
            for j in range(1, rows // HD):
                weight_sum = weight_sum + weights[:, j * HD : (j + 1) * HD]
            den_ref[h] += weight_sum
            num_ref[h] += jnp.dot(
                weights.astype(jnp.bfloat16), held[s, :, HD:], preferred_element_type=jnp.float32
            )

    end = place if stage == 0 else PLANE
    lo = jnp.clip(lax.div(jnp.maximum(starts[0], 0), rows), 0, end)
    clear = jnp.clip(lax.div(jnp.maximum(starts[-1], 0) + rows - 1, rows), lo, end)
    for copy in copies:
        copy.wait()

    @pl.loop(lo, clear)
    def _(s):
        tile(s, True, False)

    @pl.loop(clear, end)
    def _(s):
        tile(s, False, False)

    if stage == 0:
        tile(place, True, True)
    if stage == BACK:
        for h in range(heads):
            total = jnp.sum(den_ref[h], axis=1, keepdims=True)
            out_ref[:, h * HD : (h + 1) * HD] = (num_ref[h] / total).astype(jnp.bfloat16)


def attend(stage, info, q, kvs, carry):
    rows = q.shape[0]
    heads = q.shape[1] // HD
    sums = jax.ShapeDtypeStruct((heads, rows, HD), jnp.float32)
    last = stage == BACK
    whole = pl.BlockSpec(memory_space=pltpu.VMEM)
    return pl.pallas_call(
        functools.partial(attend_kernel, rows, stage),
        in_specs=[pl.BlockSpec(memory_space=pltpu.SMEM), whole]
        + [pl.BlockSpec(memory_space=pl.ANY)] * PLANE
        + [whole] * len(carry),
        out_specs=whole if last else [whole] * 2,
        out_shape=jax.ShapeDtypeStruct(q.shape, jnp.bfloat16) if last else [sums] * 2,
        scratch_shapes=([pltpu.VMEM(sums.shape, jnp.float32)] * 2 if last else [])
        + [
            pltpu.VMEM((PLANE, rows, 2 * HD), jnp.bfloat16),
            pltpu.SemaphoreType.DMA((PLANE,)),
        ],
        compiler_params=pltpu.CompilerParams(vmem_limit_bytes=32 * 2**20),
        cost_estimate=pl.CostEstimate(
            flops=2 * 10**9, bytes_accessed=4 * 10**6, transcendentals=4 * 10**6
        ),
        name="attend",
    )(info, q, *kvs, *carry)


def out_kernel(parts, *refs):
    total = jnp.dot(refs[0][...], refs[parts][...], preferred_element_type=jnp.float32)
    for i in range(1, parts):
        total = total + jnp.dot(
            refs[i][...], refs[parts + i][...], preferred_element_type=jnp.float32
        )
    refs[2 * parts][...] = total
    refs[2 * parts + 1][...] = jnp.sum(total * total, axis=1, keepdims=True)


def out_project(heads, weights):
    rows, inner = heads[0].shape
    cols = weights[0].shape[1]
    parts = len(heads)
    tile = 256
    return pl.pallas_call(
        functools.partial(out_kernel, parts),
        grid=(rows // tile,),
        in_specs=[pl.BlockSpec((tile, inner), lambda i: (i, 0))] * parts
        + [pl.BlockSpec((inner, cols), lambda i: (0, 0), pipeline_mode=pl.Buffered(1))] * parts,
        out_specs=[
            pl.BlockSpec((tile, cols), lambda i: (i, 0)),
            pl.BlockSpec((tile, 1), lambda i: (i, 0)),
        ],
        out_shape=[
            jax.ShapeDtypeStruct((rows, cols), jnp.float32),
            jax.ShapeDtypeStruct((rows, 1), jnp.float32),
        ],
        compiler_params=pltpu.CompilerParams(vmem_limit_bytes=32 * 2**20),
        cost_estimate=pl.CostEstimate(
            flops=2 * rows * inner * parts * cols, bytes_accessed=6 * 10**6, transcendentals=0
        ),
        name="out_project",
    )(*heads, *weights)


def local(n_ctx, n_tp, tokens, norm_gain, q_weight, k_weight, v_weight, o_weight, post_gain, doc_ids, plan):
    rows, features = tokens.shape
    blocks = rows // BLK
    total_blocks = doc_ids.shape[0]
    shard = lax.axis_index("ctx")
    group = lax.axis_index("tp")
    cols = o_weight.shape[1] // n_tp

    def ctx_xor(a, m):
        return lax.ppermute(a, "ctx", [(i, i ^ m) for i in range(n_ctx)])

    def ctx_z(a, d):
        return lax.ppermute(a, "ctx", [(i, (i + d * PLANE) % n_ctx) for i in range(n_ctx)])

    def tp_xor(a, m):
        return lax.ppermute(a, "tp", [(i, i ^ m) for i in range(n_tp)])

    own_kv = project(tokens, norm_gain, [k_weight, v_weight], None, "project_kv", 56)

    kvs = []
    near = own_kv
    for back in range(BACK + 1):
        near = near if back == 0 else ctx_z(near, 1)
        across = ctx_xor(near, 2)
        kvs.append([near, ctx_xor(near, 1), across, ctx_xor(across, 1)])
    queries = project(tokens, norm_gain, [q_weight], query_scale, "project_q", 40)

    first_block = jnp.sum((doc_ids[None, :] < doc_ids[:, None]).astype(jnp.int32), axis=1)
    own_first = lax.dynamic_slice_in_dim(first_block, shard * blocks, blocks, 0)
    plane_first = (shard // PLANE - BACK) * PLANE * blocks
    info = jnp.concatenate(
        [(shard % PLANE).reshape(1), (own_first - plane_first) * BLK]
    ).astype(jnp.int32)

    same = (plan[None, :] == plan[:, None]).astype(jnp.int32)
    block_ids = jnp.arange(total_blocks, dtype=jnp.int32)
    rank = jnp.sum(same * (block_ids[None, :] < block_ids[:, None]), axis=1)
    target = plan * blocks + rank
    picker = (target[None, :] == block_ids[:, None]).astype(jnp.bfloat16)

    carry = []
    for stage in range(BACK):
        carry = attend(stage, info, queries, kvs[stage], carry)

    out_weights = [
        lax.dynamic_slice_in_dim(o_weight, (group ^ m) * cols, cols, axis=1) for m in range(n_tp)
    ]
    carry, out_weights, picker = lax.optimization_barrier((carry, out_weights, picker))
    first, second = (1, 2, 3, 4), (5, 6, 7)
    for m in first:
        out_weights[m] = tp_xor(out_weights[m], m)
    natural = attend(BACK, info, queries, kvs[BACK], carry)

    width = natural.shape[1]
    piece = BLK // n_ctx
    striped = natural.reshape(blocks, n_ctx, piece, width).transpose(1, 0, 2, 3)
    striped = striped.reshape(n_ctx, blocks, piece * width)
    gathered = lax.all_to_all(striped, "ctx", 0, 0, tiled=True)
    gathered, out_weights = lax.optimization_barrier((gathered, out_weights))
    for m in second:
        out_weights[m] = tp_xor(out_weights[m], m)
    ordered = jnp.dot(
        picker,
        gathered.reshape(total_blocks, piece * width),
        preferred_element_type=jnp.float32,
    ).astype(jnp.bfloat16)
    placed = lax.all_to_all(
        ordered.reshape(n_ctx, blocks, piece * width), "ctx", 0, 0, tiled=True
    )
    placed, out_weights = lax.optimization_barrier((placed, out_weights))
    placed = (
        placed.reshape(n_ctx, blocks, piece, width).transpose(1, 0, 2, 3).reshape(rows, width)
    )

    heads = [placed] + [None] * (n_tp - 1)
    for m in (4, 1, 3, 2):
        heads[m] = tp_xor(placed, m)
    heads[5] = tp_xor(heads[4], 1)
    heads[7] = tp_xor(heads[4], 3)
    heads[6] = tp_xor(heads[2], 4)
    summed, squares = out_project(heads, out_weights)
    squares = squares.reshape(rows)
    squares = squares + tp_xor(squares, 4)
    squares = squares + tp_xor(squares, 1) + tp_xor(squares, 3) + tp_xor(squares, 2)
    scale = lax.rsqrt(squares / features + norm_eps)
    return (summed * scale[:, None] * post_gain).astype(jnp.bfloat16)


def solution(mesh):
    placed = (
        P("ctx", None),
        P(),
        P(None, "tp"),
        P(None, "tp"),
        P(None, "tp"),
        P("tp", None),
        P("tp"),
        P(),
        P(),
    )
    return jax.shard_map(
        functools.partial(local, mesh.shape["ctx"], mesh.shape["tp"]),
        mesh=mesh,
        in_specs=placed,
        out_specs=P("ctx", "tp"),
        check_vma=False,
    )
```

```python
import functools
import math

import jax
import jax.numpy as jnp
from jax import lax
from jax.experimental import pallas as pl
from jax.experimental.pallas import tpu as pltpu
from jax.sharding import PartitionSpec as P

HD = 128
BLK = 128
PLANE = 4
BACK = 2

query_scale = 144.0 ** (-0.5)
soft_cap = 50.0
norm_eps = 1e-06
LOG2E = math.log2(math.e)


def project_kernel(scale, tile, count, parts, core_ref, x_hbm, g_ref, *refs):
    w_hbms, refs = refs[:count], refs[count:]
    o_hbm, refs = (refs[0], refs[1:]) if parts else (None, refs)
    out_ref, cut_refs, refs = refs[0], refs[1 : 1 + parts // 2], refs[1 + parts // 2 :]
    x_buf, normed_buf, w_buf, x_sems, w_sems, *cut_sems = refs
    tiles = x_buf.shape[0] // tile

    def span(i):
        return pl.ds(pl.multiple_of(i * tile, tile), tile)

    def x_copy(i):
        return pltpu.make_async_copy(x_hbm.at[span(i)], x_buf.at[span(i)], x_sems.at[i])

    width = w_buf.shape[1] // count
    w_copies = [
        pltpu.make_async_copy(
            w_hbms[j], w_buf.at[:, j * width : (j + 1) * width], w_sems.at[j]
        )
        for j in range(count)
    ]
    for i in range(tiles):
        x_copy(i).start()
    for copy in w_copies:
        copy.start()
    cuts = []
    if parts:
        core, group = core_ref[0], core_ref[1]
        half, wide = cut_refs[0].shape[1:]
        cols = o_hbm.shape[1] // parts
        for m in range(parts):
            first = lax.div((group ^ m) * cols, HD) * HD
            cuts.append(
                pltpu.make_async_copy(
                    o_hbm.at[
                        pl.ds(pl.multiple_of(core * half, half), half),
                        pl.ds(pl.multiple_of(first, HD), wide),
                    ],
                    cut_refs[m % (parts // 2)].at[m // (parts // 2)],
                    cut_sems[0].at[m],
                )
            )
            cuts[-1].start()
    gain = g_ref[...].reshape(1, -1)

    @pl.loop(0, tiles)
    def _(i):
        x_copy(i).wait()
        x = x_buf[span(i)].astype(jnp.float32)
        r = lax.rsqrt(jnp.mean(x * x, axis=1, keepdims=True) + norm_eps)
        normed_buf[span(i)] = (x * r * gain).astype(jnp.bfloat16)

    for copy in w_copies:
        copy.wait()
    done = jnp.dot(normed_buf[...], w_buf[...], preferred_element_type=jnp.float32)
    if scale is not None:
        done = done * scale
    out_ref[...] = done.astype(jnp.bfloat16)
    for copy in cuts:
        copy.wait()


def project(core, tokens, gain, weights, scale, name, o_weight=None, parts=0):
    rows, d = tokens.shape
    tile = 64
    count = len(weights)
    width = sum(w.shape[1] for w in weights)
    anywhere = pl.BlockSpec(memory_space=pl.ANY)
    whole = pl.BlockSpec(memory_space=pltpu.VMEM)
    out_specs = [whole]
    out_shape = [jax.ShapeDtypeStruct((rows, width), jnp.bfloat16)]
    sems = [pltpu.SemaphoreType.DMA((rows // tile,)), pltpu.SemaphoreType.DMA((count,))]
    operands = [core, tokens, gain, *weights]
    if parts:
        wide = -(-(o_weight.shape[1] // parts) // HD) * HD
        out_specs += [whole] * (parts // 2)
        out_shape += [
            jax.ShapeDtypeStruct((2, o_weight.shape[0] // 2, wide), jnp.bfloat16)
        ] * (parts // 2)
        sems.append(pltpu.SemaphoreType.DMA((parts,)))
        operands.append(o_weight)
    return pl.pallas_call(
        functools.partial(project_kernel, scale, tile, count, parts),
        in_specs=[pl.BlockSpec(memory_space=pltpu.SMEM), anywhere, whole]
        + [anywhere] * (len(operands) - 3),
        out_specs=out_specs,
        out_shape=out_shape,
        scratch_shapes=[
            pltpu.VMEM((rows, d), jnp.bfloat16),
            pltpu.VMEM((rows, d), jnp.bfloat16),
            pltpu.VMEM((d, width), jnp.bfloat16),
        ]
        + sems,
        compiler_params=pltpu.CompilerParams(vmem_limit_bytes=56 * 2**20),
        cost_estimate=pl.CostEstimate(
            flops=2 * rows * d * width, bytes_accessed=2 * d * (rows + width), transcendentals=0
        ),
        name=name,
    )(*operands)


def attend_kernel(rows, stage, info_ref, q_ref, *refs):
    kv_refs, refs = refs[:PLANE], refs[PLANE:]
    if stage == 0:
        num_ref, den_ref, held, sems = refs
    elif stage < BACK:
        num_in, den_in, num_ref, den_ref, held, sems = refs
    else:
        num_in, den_in, out_ref, num_ref, den_ref, held, sems = refs
    place = info_ref[0]
    copies = [
        pltpu.make_async_copy(kv_refs[i], held.at[place ^ i], sems.at[i]) for i in range(PLANE)
    ]
    for copy in copies:
        copy.start()
    if stage == 0:
        num_ref[...] = jnp.zeros_like(num_ref)
        den_ref[...] = jnp.zeros_like(den_ref)
    else:
        num_ref[...] = num_in[...]
        den_ref[...] = den_in[...]
    blocks = rows // BLK
    heads = num_ref.shape[0]
    base = (BACK - stage) * PLANE
    starts = [info_ref[1 + b] - base * rows for b in range(blocks)]
    row = lax.broadcasted_iota(jnp.int32, (rows, 1), 0)
    start_row = jnp.full((rows, 1), starts[0], jnp.int32)
    for b in range(1, blocks):
        start_row = jnp.where(row >= b * BLK, starts[b], start_row)

    def tile(s, lower, causal):
        for h in range(heads):
            scores = lax.dot_general(
                q_ref[:, h * HD : (h + 1) * HD],
                held[s, :, :HD],
                (((1,), (1,)), ((), ())),
                preferred_element_type=jnp.float32,
            )
            capped = jnp.tanh(scores * (1.0 / soft_cap)) * (soft_cap * LOG2E)
            weights = jnp.exp2(capped)
            if lower or causal:
                offset = lax.broadcasted_iota(jnp.int32, (rows, rows), 1)
                allowed = offset >= start_row - s * rows
                if causal:
                    allowed = allowed & (offset <= row)
                weights = jnp.where(allowed, weights, 0.0)
            weight_sum = weights[:, :HD]
            for j in range(1, rows // HD):
                weight_sum = weight_sum + weights[:, j * HD : (j + 1) * HD]
            den_ref[h] += weight_sum
            num_ref[h] += jnp.dot(
                weights.astype(jnp.bfloat16), held[s, :, HD:], preferred_element_type=jnp.float32
            )

    end = place if stage == 0 else PLANE
    lo = jnp.clip(lax.div(jnp.maximum(starts[0], 0), rows), 0, end)
    clear = jnp.clip(lax.div(jnp.maximum(starts[-1], 0) + rows - 1, rows), lo, end)
    for copy in copies:
        copy.wait()

    @pl.loop(lo, clear)
    def _(s):
        tile(s, True, False)

    @pl.loop(clear, end)
    def _(s):
        tile(s, False, False)

    if stage == 0:
        tile(place, True, True)
    if stage == BACK:
        for h in range(heads):
            total = jnp.sum(den_ref[h], axis=1, keepdims=True)
            out_ref[:, h * HD : (h + 1) * HD] = (num_ref[h] / total).astype(jnp.bfloat16)


def attend(stage, info, q, kvs, carry):
    rows = q.shape[0]
    heads = q.shape[1] // HD
    sums = jax.ShapeDtypeStruct((heads, rows, HD), jnp.float32)
    last = stage == BACK
    whole = pl.BlockSpec(memory_space=pltpu.VMEM)
    return pl.pallas_call(
        functools.partial(attend_kernel, rows, stage),
        in_specs=[pl.BlockSpec(memory_space=pltpu.SMEM), whole]
        + [pl.BlockSpec(memory_space=pl.ANY)] * PLANE
        + [whole] * len(carry),
        out_specs=whole if last else [whole] * 2,
        out_shape=jax.ShapeDtypeStruct(q.shape, jnp.bfloat16) if last else [sums] * 2,
        scratch_shapes=([pltpu.VMEM(sums.shape, jnp.float32)] * 2 if last else [])
        + [
            pltpu.VMEM((PLANE, rows, 2 * HD), jnp.bfloat16),
            pltpu.SemaphoreType.DMA((PLANE,)),
        ],
        compiler_params=pltpu.CompilerParams(vmem_limit_bytes=32 * 2**20),
        cost_estimate=pl.CostEstimate(
            flops=2 * 10**9, bytes_accessed=4 * 10**6, transcendentals=4 * 10**6
        ),
        name="attend",
    )(info, q, *kvs, *carry)


def out_kernel(parts, cols, info_ref, *refs):
    count = 4
    w_refs, head_refs, (sum_ref, square_ref, lhs) = (
        refs[:count],
        refs[count : count + parts],
        refs[count + parts :],
    )
    core, group = info_ref[0], info_ref[1]
    groups, half, wide = w_refs[0].shape
    for m in range(parts):
        for i, side in enumerate((core, 1 - core)):
            span = pl.ds(pl.multiple_of(side * half, half), half)
            lhs[2 * i + m // groups, :, m % groups * half : (m % groups + 1) * half] = (
                head_refs[m][:, span]
            )
    total = None
    for i in range(count):
        product = jnp.dot(
            lhs[i],
            w_refs[i][...].reshape(groups * half, wide),
            preferred_element_type=jnp.float32,
        )
        total = product if total is None else total + product
    total = jnp.where(group % 2 == 1, total[:, wide - cols :], total[:, :cols])
    sum_ref[...] = total
    square = total * total
    high = square.astype(jnp.bfloat16)
    low = (square - high.astype(jnp.float32)).astype(jnp.bfloat16)
    ones = jnp.ones((16, cols), jnp.bfloat16)
    sums = None
    for part in (high, low):
        product = lax.dot_general(
            ones, part, (((1,), (1,)), ((), ())), preferred_element_type=jnp.float32
        )
        sums = product if sums is None else sums + product
    square_ref[...] = sums[:1]


def out_project(info, heads, weights, cols):
    rows, inner = heads[0].shape
    parts = len(heads)
    whole = pl.BlockSpec(memory_space=pltpu.VMEM)
    return pl.pallas_call(
        functools.partial(out_kernel, parts, cols),
        in_specs=[pl.BlockSpec(memory_space=pltpu.SMEM)] + [whole] * (parts + len(weights)),
        out_specs=[whole] * 2,
        out_shape=[
            jax.ShapeDtypeStruct((rows, cols), jnp.float32),
            jax.ShapeDtypeStruct((1, rows), jnp.float32),
        ],
        scratch_shapes=[pltpu.VMEM((len(weights), rows, parts * inner // 4), jnp.bfloat16)],
        compiler_params=pltpu.CompilerParams(vmem_limit_bytes=32 * 2**20),
        cost_estimate=pl.CostEstimate(
            flops=2 * rows * inner * parts * cols, bytes_accessed=6 * 10**6, transcendentals=0
        ),
        name="out_project",
    )(info, *weights, *heads)


def local(n_ctx, n_tp, tokens, norm_gain, q_weight, k_weight, v_weight, o_weight, post_gain, doc_ids, plan):
    rows, features = tokens.shape
    blocks = rows // BLK
    total_blocks = doc_ids.shape[0]
    shard = lax.axis_index("ctx")
    group = lax.axis_index("tp")
    cols = o_weight.shape[1] // n_tp
    core = shard % 2

    def ctx_xor(a, m):
        return lax.ppermute(a, "ctx", [(i, i ^ m) for i in range(n_ctx)])

    def ctx_z(a, d):
        return lax.ppermute(a, "ctx", [(i, (i + d * PLANE) % n_ctx) for i in range(n_ctx)])

    def tp_xor(a, m):
        return lax.ppermute(a, "tp", [(i, i ^ m) for i in range(n_tp)])

    which = jnp.stack([core, group]).astype(jnp.int32)
    own_kv, *cuts = project(
        which, tokens, norm_gain, [k_weight, v_weight], None, "project_kv", o_weight, n_tp
    )
    (queries,) = project(which, tokens, norm_gain, [q_weight], query_scale, "project_q")
    cuts = [c if m == 0 else tp_xor(c, m) for m, c in enumerate(cuts)]
    mine = jnp.stack([c[0] for c in cuts])
    passed = jnp.stack([c[1] for c in cuts])

    first_block = jnp.sum((doc_ids[None, :] < doc_ids[:, None]).astype(jnp.int32), axis=1)
    own_first = lax.dynamic_slice_in_dim(first_block, shard * blocks, blocks, 0)
    plane_first = (shard // PLANE - BACK) * PLANE * blocks
    info = jnp.concatenate(
        [(shard % PLANE).reshape(1), (own_first - plane_first) * BLK]
    ).astype(jnp.int32)

    same = (plan[None, :] == plan[:, None]).astype(jnp.int32)
    block_ids = jnp.arange(total_blocks, dtype=jnp.int32)
    rank = jnp.sum(same * (block_ids[None, :] < block_ids[:, None]), axis=1)
    target = plan * blocks + rank
    picker = (target[None, :] == block_ids[:, None]).astype(jnp.bfloat16)

    back_one = ctx_z(own_kv, 1)
    back_two = ctx_z(back_one, 1)
    across = [ctx_xor(near, 2) for near in (own_kv, back_one, back_two)]
    carry = []
    for stage, near in enumerate((own_kv, back_one)):
        kvs = [near, ctx_xor(near, 1), across[stage], ctx_xor(across[stage], 1)]
        carry = attend(stage, info, queries, kvs, carry)
    far, carry, mine, passed, picker = lax.optimization_barrier(
        (across[BACK], carry, mine, passed, picker)
    )
    passed = tp_xor(passed, n_tp // 2)
    kvs = [back_two, ctx_xor(back_two, 1), far, ctx_xor(far, 1)]
    natural = attend(BACK, info, queries, kvs, carry)

    width = natural.shape[1]
    piece = BLK // n_ctx
    striped = natural.reshape(blocks, n_ctx, piece, width).transpose(1, 0, 2, 3)
    striped = striped.reshape(n_ctx, blocks, piece * width)
    gathered = lax.all_to_all(striped, "ctx", 0, 0, tiled=True)
    gathered, mine, passed = lax.optimization_barrier((gathered, mine, passed))
    weights = [mine, passed, ctx_xor(mine, 1), ctx_xor(passed, 1)]
    ordered = jnp.dot(
        picker,
        gathered.reshape(total_blocks, piece * width),
        preferred_element_type=jnp.float32,
    ).astype(jnp.bfloat16)
    placed = lax.all_to_all(
        ordered.reshape(n_ctx, blocks, piece * width), "ctx", 0, 0, tiled=True
    )
    placed = (
        placed.reshape(n_ctx, blocks, piece, width).transpose(1, 0, 2, 3).reshape(rows, width)
    )

    heads = [placed] + [None] * (n_tp - 1)
    for m in (4, 1, 3, 2):
        heads[m] = tp_xor(placed, m)
    heads[5] = tp_xor(heads[4], 1)
    heads[7] = tp_xor(heads[4], 3)
    heads[6] = tp_xor(heads[2], 4)
    summed, squares = out_project(which, heads, weights, cols)
    squares = squares.reshape(rows)
    squares = squares + tp_xor(squares, 4)
    squares = squares + tp_xor(squares, 1) + tp_xor(squares, 3) + tp_xor(squares, 2)
    scale = lax.rsqrt(squares / features + norm_eps)
    return (summed * scale[:, None] * post_gain).astype(jnp.bfloat16)


def solution(mesh):
    placed = (
        P("ctx", None),
        P(),
        P(None, "tp"),
        P(None, "tp"),
        P(None, "tp"),
        P("tp", None),
        P("tp"),
        P(),
        P(),
    )
    return jax.shard_map(
        functools.partial(local, mesh.shape["ctx"], mesh.shape["tp"]),
        mesh=mesh,
        in_specs=placed,
        out_specs=P("ctx", "tp"),
        check_vma=False,
    )
```

```python
import functools
import math

import jax
import jax.numpy as jnp
from jax import lax
from jax.experimental import pallas as pl
from jax.experimental.pallas import tpu as pltpu
from jax.sharding import PartitionSpec as P

HD = 128
BLK = 128
PLANE = 4
BACK = 2

query_scale = 144.0 ** (-0.5)
soft_cap = 50.0
norm_eps = 1e-06
LOG2E = math.log2(math.e)


def project_kernel(scale, tile, count, parts, core_ref, x_hbm, g_ref, *refs):
    w_hbms, refs = refs[:count], refs[count:]
    o_hbm, refs = (refs[0], refs[1:]) if parts else (None, refs)
    out_ref, cut_refs, refs = refs[0], refs[1 : 1 + parts // 2], refs[1 + parts // 2 :]
    x_buf, normed_buf, w_buf, x_sems, w_sems, *cut_sems = refs
    tiles = x_buf.shape[0] // tile

    def span(i):
        return pl.ds(pl.multiple_of(i * tile, tile), tile)

    def x_copy(i):
        return pltpu.make_async_copy(x_hbm.at[span(i)], x_buf.at[span(i)], x_sems.at[i])

    width = w_buf.shape[1] // count
    w_copies = [
        pltpu.make_async_copy(
            w_hbms[j], w_buf.at[:, j * width : (j + 1) * width], w_sems.at[j]
        )
        for j in range(count)
    ]
    for i in range(tiles):
        x_copy(i).start()
    for copy in w_copies:
        copy.start()
    cuts = []
    if parts:
        core, group = core_ref[0], core_ref[1]
        half, wide = cut_refs[0].shape[1:]
        cols = o_hbm.shape[1] // parts
        for m in range(parts):
            first = lax.div((group ^ m) * cols, HD) * HD
            cuts.append(
                pltpu.make_async_copy(
                    o_hbm.at[
                        pl.ds(pl.multiple_of(core * half, half), half),
                        pl.ds(pl.multiple_of(first, HD), wide),
                    ],
                    cut_refs[m % (parts // 2)].at[m // (parts // 2)],
                    cut_sems[0].at[m],
                )
            )
            cuts[-1].start()
    gain = g_ref[...].reshape(1, -1)

    @pl.loop(0, tiles)
    def _(i):
        x_copy(i).wait()
        x = x_buf[span(i)].astype(jnp.float32)
        r = lax.rsqrt(jnp.mean(x * x, axis=1, keepdims=True) + norm_eps)
        normed_buf[span(i)] = (x * r * gain).astype(jnp.bfloat16)

    for copy in w_copies:
        copy.wait()
    done = jnp.dot(normed_buf[...], w_buf[...], preferred_element_type=jnp.float32)
    if scale is not None:
        done = done * scale
    out_ref[...] = done.astype(jnp.bfloat16)
    for copy in cuts:
        copy.wait()


def project(core, tokens, gain, weights, scale, name, o_weight=None, parts=0):
    rows, d = tokens.shape
    tile = 64
    count = len(weights)
    width = sum(w.shape[1] for w in weights)
    anywhere = pl.BlockSpec(memory_space=pl.ANY)
    whole = pl.BlockSpec(memory_space=pltpu.VMEM)
    out_specs = [whole]
    out_shape = [jax.ShapeDtypeStruct((rows, width), jnp.bfloat16)]
    sems = [pltpu.SemaphoreType.DMA((rows // tile,)), pltpu.SemaphoreType.DMA((count,))]
    operands = [core, tokens, gain, *weights]
    if parts:
        wide = -(-(o_weight.shape[1] // parts) // HD) * HD
        out_specs += [whole] * (parts // 2)
        out_shape += [
            jax.ShapeDtypeStruct((2, o_weight.shape[0] // 2, wide), jnp.bfloat16)
        ] * (parts // 2)
        sems.append(pltpu.SemaphoreType.DMA((parts,)))
        operands.append(o_weight)
    return pl.pallas_call(
        functools.partial(project_kernel, scale, tile, count, parts),
        in_specs=[pl.BlockSpec(memory_space=pltpu.SMEM), anywhere, whole]
        + [anywhere] * (len(operands) - 3),
        out_specs=out_specs,
        out_shape=out_shape,
        scratch_shapes=[
            pltpu.VMEM((rows, d), jnp.bfloat16),
            pltpu.VMEM((rows, d), jnp.bfloat16),
            pltpu.VMEM((d, width), jnp.bfloat16),
        ]
        + sems,
        compiler_params=pltpu.CompilerParams(vmem_limit_bytes=56 * 2**20),
        cost_estimate=pl.CostEstimate(
            flops=2 * rows * d * width, bytes_accessed=2 * d * (rows + width), transcendentals=0
        ),
        name=name,
    )(*operands)


def attend_kernel(rows, stage, info_ref, q_ref, *refs):
    kv_refs, refs = refs[:PLANE], refs[PLANE:]
    if stage == 0:
        num_ref, den_ref, held, sems = refs
    elif stage < BACK:
        num_in, den_in, num_ref, den_ref, held, sems = refs
    else:
        num_in, den_in, out_ref, num_ref, den_ref, held, sems = refs
    place = info_ref[0]
    copies = [
        pltpu.make_async_copy(kv_refs[i], held.at[place ^ i], sems.at[i]) for i in range(PLANE)
    ]
    for copy in copies:
        copy.start()
    if stage == 0:
        num_ref[...] = jnp.zeros_like(num_ref)
        den_ref[...] = jnp.zeros_like(den_ref)
    else:
        num_ref[...] = num_in[...]
        den_ref[...] = den_in[...]
    blocks = rows // BLK
    heads = num_ref.shape[0]
    base = (BACK - stage) * PLANE
    starts = [info_ref[1 + b] - base * rows for b in range(blocks)]
    row = lax.broadcasted_iota(jnp.int32, (rows, 1), 0)
    start_row = jnp.full((rows, 1), starts[0], jnp.int32)
    for b in range(1, blocks):
        start_row = jnp.where(row >= b * BLK, starts[b], start_row)

    def tile(s, lower, causal):
        for h in range(heads):
            scores = lax.dot_general(
                q_ref[:, h * HD : (h + 1) * HD],
                held[s, :, :HD],
                (((1,), (1,)), ((), ())),
                preferred_element_type=jnp.float32,
            )
            capped = jnp.tanh(scores * (1.0 / soft_cap)) * (soft_cap * LOG2E)
            weights = jnp.exp2(capped)
            if lower or causal:
                offset = lax.broadcasted_iota(jnp.int32, (rows, rows), 1)
                allowed = offset >= start_row - s * rows
                if causal:
                    allowed = allowed & (offset <= row)
                weights = jnp.where(allowed, weights, 0.0)
            weight_sum = weights[:, :HD]
            for j in range(1, rows // HD):
                weight_sum = weight_sum + weights[:, j * HD : (j + 1) * HD]
            den_ref[h] += weight_sum
            num_ref[h] += jnp.dot(
                weights.astype(jnp.bfloat16), held[s, :, HD:], preferred_element_type=jnp.float32
            )

    end = place if stage == 0 else PLANE
    lo = jnp.clip(lax.div(jnp.maximum(starts[0], 0), rows), 0, end)
    clear = jnp.clip(lax.div(jnp.maximum(starts[-1], 0) + rows - 1, rows), lo, end)
    for copy in copies:
        copy.wait()

    @pl.loop(lo, clear)
    def _(s):
        tile(s, True, False)

    @pl.loop(clear, end)
    def _(s):
        tile(s, False, False)

    if stage == 0:
        tile(place, True, True)
    if stage == BACK:
        for h in range(heads):
            total = jnp.sum(den_ref[h], axis=1, keepdims=True)
            out_ref[:, h * HD : (h + 1) * HD] = (num_ref[h] / total).astype(jnp.bfloat16)


def attend(stage, info, q, kvs, carry):
    rows = q.shape[0]
    heads = q.shape[1] // HD
    sums = jax.ShapeDtypeStruct((heads, rows, HD), jnp.float32)
    last = stage == BACK
    whole = pl.BlockSpec(memory_space=pltpu.VMEM)
    return pl.pallas_call(
        functools.partial(attend_kernel, rows, stage),
        in_specs=[pl.BlockSpec(memory_space=pltpu.SMEM), whole]
        + [pl.BlockSpec(memory_space=pl.ANY)] * PLANE
        + [whole] * len(carry),
        out_specs=whole if last else [whole] * 2,
        out_shape=jax.ShapeDtypeStruct(q.shape, jnp.bfloat16) if last else [sums] * 2,
        scratch_shapes=([pltpu.VMEM(sums.shape, jnp.float32)] * 2 if last else [])
        + [
            pltpu.VMEM((PLANE, rows, 2 * HD), jnp.bfloat16),
            pltpu.SemaphoreType.DMA((PLANE,)),
        ],
        compiler_params=pltpu.CompilerParams(vmem_limit_bytes=32 * 2**20),
        cost_estimate=pl.CostEstimate(
            flops=2 * 10**9, bytes_accessed=4 * 10**6, transcendentals=4 * 10**6
        ),
        name="attend",
    )(info, q, *kvs, *carry)


def out_kernel(parts, cols, places, info_ref, *refs):
    count = len(places)
    w_refs, head_refs, (sum_ref, square_ref, lhs) = (
        refs[:count],
        refs[count : count + parts],
        refs[count + parts :],
    )
    core, group = info_ref[0], info_ref[1]
    half, wide = w_refs[0].shape[1:]
    total, at = None, 0
    for w_ref, (side, members) in zip(w_refs, places):
        side = core if side == 0 else 1 - core
        span = pl.ds(pl.multiple_of(side * half, half), half)
        first = at
        for m in members:
            lhs[:, at : at + half] = head_refs[m][:, span]
            at += half
        product = jnp.dot(
            lhs[:, first:at],
            w_ref[...].reshape(at - first, wide),
            preferred_element_type=jnp.float32,
        )
        total = product if total is None else total + product
    total = jnp.where(group % 2 == 1, total[:, wide - cols :], total[:, :cols])
    sum_ref[...] = total
    square = total * total
    high = square.astype(jnp.bfloat16)
    low = (square - high.astype(jnp.float32)).astype(jnp.bfloat16)
    ones = jnp.ones((16, cols), jnp.bfloat16)
    sums = None
    for part in (high, low):
        product = lax.dot_general(
            ones, part, (((1,), (1,)), ((), ())), preferred_element_type=jnp.float32
        )
        sums = product if sums is None else sums + product
    square_ref[...] = sums[:1]


def out_project(info, heads, weights, places, cols):
    rows, inner = heads[0].shape
    parts = len(heads)
    whole = pl.BlockSpec(memory_space=pltpu.VMEM)
    return pl.pallas_call(
        functools.partial(out_kernel, parts, cols, places),
        in_specs=[pl.BlockSpec(memory_space=pltpu.SMEM)] + [whole] * (parts + len(weights)),
        out_specs=[whole] * 2,
        out_shape=[
            jax.ShapeDtypeStruct((rows, cols), jnp.float32),
            jax.ShapeDtypeStruct((1, rows), jnp.float32),
        ],
        scratch_shapes=[pltpu.VMEM((rows, parts * inner), jnp.bfloat16)],
        compiler_params=pltpu.CompilerParams(vmem_limit_bytes=32 * 2**20),
        cost_estimate=pl.CostEstimate(
            flops=2 * rows * inner * parts * cols, bytes_accessed=6 * 10**6, transcendentals=0
        ),
        name="out_project",
    )(info, *weights, *heads)


def local(n_ctx, n_tp, tokens, norm_gain, q_weight, k_weight, v_weight, o_weight, post_gain, doc_ids, plan):
    rows, features = tokens.shape
    blocks = rows // BLK
    total_blocks = doc_ids.shape[0]
    shard = lax.axis_index("ctx")
    group = lax.axis_index("tp")
    cols = o_weight.shape[1] // n_tp
    core = shard % 2

    def ctx_xor(a, m):
        return lax.ppermute(a, "ctx", [(i, i ^ m) for i in range(n_ctx)])

    def ctx_z(a, d):
        return lax.ppermute(a, "ctx", [(i, (i + d * PLANE) % n_ctx) for i in range(n_ctx)])

    def tp_xor(a, m):
        return lax.ppermute(a, "tp", [(i, i ^ m) for i in range(n_tp)])

    which = jnp.stack([core, group]).astype(jnp.int32)
    own_kv, *cuts = project(
        which, tokens, norm_gain, [k_weight, v_weight], None, "project_kv", o_weight, n_tp
    )
    (queries,) = project(which, tokens, norm_gain, [q_weight], query_scale, "project_q")
    first_block = jnp.sum((doc_ids[None, :] < doc_ids[:, None]).astype(jnp.int32), axis=1)
    own_first = lax.dynamic_slice_in_dim(first_block, shard * blocks, blocks, 0)
    plane_first = (shard // PLANE - BACK) * PLANE * blocks
    info = jnp.concatenate(
        [(shard % PLANE).reshape(1), (own_first - plane_first) * BLK]
    ).astype(jnp.int32)

    same = (plan[None, :] == plan[:, None]).astype(jnp.int32)
    block_ids = jnp.arange(total_blocks, dtype=jnp.int32)
    rank = jnp.sum(same * (block_ids[None, :] < block_ids[:, None]), axis=1)
    target = plan * blocks + rank
    picker = (target[None, :] == block_ids[:, None]).astype(jnp.bfloat16)

    planes = [own_kv, ctx_z(own_kv, 1)]
    across = [ctx_xor(own_kv, 2)]
    cuts = [tp_xor(c, m) if m % 2 else c for m, c in enumerate(cuts)]
    planes, queries, cuts[2] = lax.optimization_barrier((planes, queries, cuts[2]))
    planes.append(ctx_z(planes[1], 1))
    across += [ctx_xor(near, 2) for near in planes[1:]]
    cuts[2] = tp_xor(cuts[2], 2)
    carry = []
    for stage in range(BACK):
        near = planes[stage]
        kvs = [near, ctx_xor(near, 1), across[stage], ctx_xor(across[stage], 1)]
        carry = attend(stage, info, queries, kvs, carry)
    mine = jnp.stack([c[0] for c in cuts])
    passed = jnp.stack([c[1] for c in cuts])
    far, carry, mine, passed, picker = lax.optimization_barrier(
        (across[BACK], carry, mine, passed, picker)
    )
    passed = tp_xor(passed, n_tp // 2)
    kvs = [planes[BACK], ctx_xor(planes[BACK], 1), far, ctx_xor(far, 1)]
    natural = attend(BACK, info, queries, kvs, carry)

    width = natural.shape[1]
    piece = BLK // n_ctx
    striped = natural.reshape(blocks, n_ctx, piece, width).transpose(1, 0, 2, 3)
    striped = striped.reshape(n_ctx, blocks, piece * width)
    gathered = lax.all_to_all(striped, "ctx", 0, 0, tiled=True)
    gathered, mine, passed = lax.optimization_barrier((gathered, mine, passed))
    weights = [mine, passed, ctx_xor(mine, 1), ctx_xor(passed, 1)]
    kept, crossed = tuple(range(n_tp // 2)), tuple(range(n_tp // 2, n_tp))
    places = ((0, kept), (0, crossed), (1, kept), (1, crossed))
    ordered = jnp.dot(
        picker,
        gathered.reshape(total_blocks, piece * width),
        preferred_element_type=jnp.float32,
    ).astype(jnp.bfloat16)
    placed = lax.all_to_all(
        ordered.reshape(n_ctx, blocks, piece * width), "ctx", 0, 0, tiled=True
    )
    placed = (
        placed.reshape(n_ctx, blocks, piece, width).transpose(1, 0, 2, 3).reshape(rows, width)
    )

    heads = [placed] + [None] * (n_tp - 1)
    for m in (4, 1, 3, 2):
        heads[m] = tp_xor(placed, m)
    heads[5] = tp_xor(heads[4], 1)
    heads[7] = tp_xor(heads[4], 3)
    heads[6] = tp_xor(heads[2], 4)
    summed, squares = out_project(which, heads, weights, places, cols)
    squares = squares.reshape(rows)
    squares = squares + tp_xor(squares, 4)
    squares = squares + tp_xor(squares, 1) + tp_xor(squares, 3) + tp_xor(squares, 2)
    scale = lax.rsqrt(squares / features + norm_eps)
    return (summed * scale[:, None] * post_gain).astype(jnp.bfloat16)


def solution(mesh):
    placed = (
        P("ctx", None),
        P(),
        P(None, "tp"),
        P(None, "tp"),
        P(None, "tp"),
        P("tp", None),
        P("tp"),
        P(),
        P(),
    )
    return jax.shard_map(
        functools.partial(local, mesh.shape["ctx"], mesh.shape["tp"]),
        mesh=mesh,
        in_specs=placed,
        out_specs=P("ctx", "tp"),
        check_vma=False,
    )
```

```python
import functools
import math

import jax
import jax.numpy as jnp
from jax import lax
from jax.experimental import pallas as pl
from jax.experimental.pallas import tpu as pltpu
from jax.sharding import PartitionSpec as P

HD = 128
BLK = 128
PLANE = 4
BACK = 2

query_scale = 144.0 ** (-0.5)
soft_cap = 50.0
norm_eps = 1e-06
LOG2E = math.log2(math.e)


def project_kernel(scale, tile, count, parts, x_hbm, g_ref, *refs):
    w_hbms, refs = refs[:count], refs[count:]
    o_hbm, refs = (refs[0], refs[1:]) if parts else (None, refs)
    out_ref, cut_refs, refs = refs[0], refs[1 : 1 + parts // 2], refs[1 + parts // 2 :]
    x_buf, normed_buf, w_buf, x_sems, w_sems, *cut_sems = refs
    tiles = x_buf.shape[0] // tile

    def span(i):
        return pl.ds(pl.multiple_of(i * tile, tile), tile)

    def x_copy(i):
        return pltpu.make_async_copy(x_hbm.at[span(i)], x_buf.at[span(i)], x_sems.at[i])

    width = w_buf.shape[1] // count
    w_copies = [
        pltpu.make_async_copy(
            w_hbms[j], w_buf.at[:, j * width : (j + 1) * width], w_sems.at[j]
        )
        for j in range(count)
    ]
    for i in range(tiles):
        x_copy(i).start()
    for copy in w_copies:
        copy.start()
    cuts = []
    if parts:
        core, group = lax.rem(lax.axis_index("ctx"), 2), lax.axis_index("tp")
        half, wide = cut_refs[0].shape[1:]
        cols = o_hbm.shape[1] // parts
        for m in range(parts):
            first = lax.div((group ^ m) * cols, HD) * HD
            cuts.append(
                pltpu.make_async_copy(
                    o_hbm.at[
                        pl.ds(pl.multiple_of(core * half, half), half),
                        pl.ds(pl.multiple_of(first, HD), wide),
                    ],
                    cut_refs[m % (parts // 2)].at[m // (parts // 2)],
                    cut_sems[0].at[m],
                )
            )
            cuts[-1].start()
    gain = g_ref[...].reshape(1, -1)

    @pl.loop(0, tiles)
    def _(i):
        x_copy(i).wait()
        x = x_buf[span(i)].astype(jnp.float32)
        r = lax.rsqrt(jnp.mean(x * x, axis=1, keepdims=True) + norm_eps)
        normed_buf[span(i)] = (x * r * gain).astype(jnp.bfloat16)

    for copy in w_copies:
        copy.wait()
    done = jnp.dot(normed_buf[...], w_buf[...], preferred_element_type=jnp.float32)
    if scale is not None:
        done = done * scale
    out_ref[...] = done.astype(jnp.bfloat16)
    for copy in cuts:
        copy.wait()


def project(tokens, gain, weights, scale, name, o_weight=None, parts=0):
    rows, d = tokens.shape
    tile = 64
    count = len(weights)
    width = sum(w.shape[1] for w in weights)
    anywhere = pl.BlockSpec(memory_space=pl.ANY)
    whole = pl.BlockSpec(memory_space=pltpu.VMEM)
    out_specs = [whole]
    out_shape = [jax.ShapeDtypeStruct((rows, width), jnp.bfloat16)]
    sems = [pltpu.SemaphoreType.DMA((rows // tile,)), pltpu.SemaphoreType.DMA((count,))]
    operands = [tokens, gain, *weights]
    if parts:
        wide = -(-(o_weight.shape[1] // parts) // HD) * HD
        out_specs += [whole] * (parts // 2)
        out_shape += [
            jax.ShapeDtypeStruct((2, o_weight.shape[0] // 2, wide), jnp.bfloat16)
        ] * (parts // 2)
        sems.append(pltpu.SemaphoreType.DMA((parts,)))
        operands.append(o_weight)
    return pl.pallas_call(
        functools.partial(project_kernel, scale, tile, count, parts),
        in_specs=[anywhere, whole] + [anywhere] * (len(operands) - 2),
        out_specs=out_specs,
        out_shape=out_shape,
        scratch_shapes=[
            pltpu.VMEM((rows, d), jnp.bfloat16),
            pltpu.VMEM((rows, d), jnp.bfloat16),
            pltpu.VMEM((d, width), jnp.bfloat16),
        ]
        + sems,
        compiler_params=pltpu.CompilerParams(vmem_limit_bytes=56 * 2**20),
        cost_estimate=pl.CostEstimate(
            flops=2 * rows * d * width, bytes_accessed=2 * d * (rows + width), transcendentals=0
        ),
        name=name,
    )(*operands)


def attend_kernel(rows, stage, info_ref, q_ref, *refs):
    kv_refs, refs = refs[:PLANE], refs[PLANE:]
    if stage == 0:
        num_ref, den_ref, held, sems = refs
    elif stage < BACK:
        num_in, den_in, num_ref, den_ref, held, sems = refs
    else:
        num_in, den_in, out_ref, num_ref, den_ref, held, sems = refs
    place = info_ref[0]
    copies = [
        pltpu.make_async_copy(kv_refs[i], held.at[place ^ i], sems.at[i]) for i in range(PLANE)
    ]
    for copy in copies:
        copy.start()
    if stage == 0:
        num_ref[...] = jnp.zeros_like(num_ref)
        den_ref[...] = jnp.zeros_like(den_ref)
    else:
        num_ref[...] = num_in[...]
        den_ref[...] = den_in[...]
    blocks = rows // BLK
    heads = num_ref.shape[0]
    base = (BACK - stage) * PLANE
    starts = [info_ref[1 + b] - base * rows for b in range(blocks)]
    row = lax.broadcasted_iota(jnp.int32, (rows, 1), 0)
    start_row = jnp.full((rows, 1), starts[0], jnp.int32)
    for b in range(1, blocks):
        start_row = jnp.where(row >= b * BLK, starts[b], start_row)

    def tile(s, lower, causal):
        for h in range(heads):
            scores = lax.dot_general(
                q_ref[:, h * HD : (h + 1) * HD],
                held[s, :, :HD],
                (((1,), (1,)), ((), ())),
                preferred_element_type=jnp.float32,
            )
            capped = jnp.tanh(scores * (1.0 / soft_cap)) * (soft_cap * LOG2E)
            weights = jnp.exp2(capped)
            if lower or causal:
                offset = lax.broadcasted_iota(jnp.int32, (rows, rows), 1)
                allowed = offset >= start_row - s * rows
                if causal:
                    allowed = allowed & (offset <= row)
                weights = jnp.where(allowed, weights, 0.0)
            weight_sum = weights[:, :HD]
            for j in range(1, rows // HD):
                weight_sum = weight_sum + weights[:, j * HD : (j + 1) * HD]
            den_ref[h] += weight_sum
            num_ref[h] += jnp.dot(
                weights.astype(jnp.bfloat16), held[s, :, HD:], preferred_element_type=jnp.float32
            )

    end = place if stage == 0 else PLANE
    lo = jnp.clip(lax.div(jnp.maximum(starts[0], 0), rows), 0, end)
    clear = jnp.clip(lax.div(jnp.maximum(starts[-1], 0) + rows - 1, rows), lo, end)
    for copy in copies:
        copy.wait()

    @pl.loop(lo, clear)
    def _(s):
        tile(s, True, False)

    @pl.loop(clear, end)
    def _(s):
        tile(s, False, False)

    if stage == 0:
        tile(place, True, True)
    if stage == BACK:
        for h in range(heads):
            total = jnp.sum(den_ref[h], axis=1, keepdims=True)
            out_ref[:, h * HD : (h + 1) * HD] = (num_ref[h] / total).astype(jnp.bfloat16)


def attend(stage, info, q, kvs, carry):
    rows = q.shape[0]
    heads = q.shape[1] // HD
    sums = jax.ShapeDtypeStruct((heads, rows, HD), jnp.float32)
    last = stage == BACK
    whole = pl.BlockSpec(memory_space=pltpu.VMEM)
    return pl.pallas_call(
        functools.partial(attend_kernel, rows, stage),
        in_specs=[pl.BlockSpec(memory_space=pltpu.SMEM), whole]
        + [pl.BlockSpec(memory_space=pl.ANY)] * PLANE
        + [whole] * len(carry),
        out_specs=whole if last else [whole] * 2,
        out_shape=jax.ShapeDtypeStruct(q.shape, jnp.bfloat16) if last else [sums] * 2,
        scratch_shapes=([pltpu.VMEM(sums.shape, jnp.float32)] * 2 if last else [])
        + [
            pltpu.VMEM((PLANE, rows, 2 * HD), jnp.bfloat16),
            pltpu.SemaphoreType.DMA((PLANE,)),
        ],
        compiler_params=pltpu.CompilerParams(vmem_limit_bytes=32 * 2**20),
        cost_estimate=pl.CostEstimate(
            flops=2 * 10**9, bytes_accessed=4 * 10**6, transcendentals=4 * 10**6
        ),
        name="attend",
    )(info, q, *kvs, *carry)


def out_kernel(heads, cols, places, *refs):
    count = len(places)
    w_refs, refs = refs[:count], refs[count:]
    head_refs, refs = refs[:heads], refs[heads:]
    total = None
    if cols:
        before_ref, sum_ref, square_ref, lhs = refs
        total = before_ref[...]
    else:
        sum_ref, lhs = refs
    core, group = lax.rem(lax.axis_index("ctx"), 2), lax.axis_index("tp")
    half, wide = w_refs[0].shape[1:]
    at = 0
    for w_ref, (side, first_group, members) in zip(w_refs, places):
        side = core if side == 0 else 1 - core
        span = pl.ds(pl.multiple_of(side * half, half), half)
        first = at
        for m in members:
            lhs[:, at : at + half] = head_refs[m][:, span]
            at += half
        product = jnp.dot(
            lhs[:, first:at],
            w_ref[first_group : first_group + len(members)].reshape(at - first, wide),
            preferred_element_type=jnp.float32,
        )
        total = product if total is None else total + product
    if not cols:
        sum_ref[...] = total
        return
    total = jnp.where(group % 2 == 1, total[:, wide - cols :], total[:, :cols])
    sum_ref[...] = total
    square = total * total
    high = square.astype(jnp.bfloat16)
    low = (square - high.astype(jnp.float32)).astype(jnp.bfloat16)
    ones = jnp.ones((16, cols), jnp.bfloat16)
    sums = None
    for part in (high, low):
        product = lax.dot_general(
            ones, part, (((1,), (1,)), ((), ())), preferred_element_type=jnp.float32
        )
        sums = product if sums is None else sums + product
    square_ref[...] = sums[:1]


def out_project(heads, weights, places, before=None, cols=0):
    rows, inner = heads[0].shape
    wide = weights[0].shape[2]
    whole = pl.BlockSpec(memory_space=pltpu.VMEM)
    if cols:
        out_shape = [
            jax.ShapeDtypeStruct((rows, cols), jnp.float32),
            jax.ShapeDtypeStruct((1, rows), jnp.float32),
        ]
        extra = [before]
    else:
        out_shape = [jax.ShapeDtypeStruct((rows, wide), jnp.float32)]
        extra = []
    return pl.pallas_call(
        functools.partial(out_kernel, len(heads), cols, places),
        in_specs=[whole] * (len(heads) + len(weights) + len(extra)),
        out_specs=[whole] * len(out_shape),
        out_shape=out_shape,
        scratch_shapes=[pltpu.VMEM((rows, len(heads) * inner), jnp.bfloat16)],
        compiler_params=pltpu.CompilerParams(vmem_limit_bytes=32 * 2**20),
        cost_estimate=pl.CostEstimate(
            flops=2 * rows * inner * len(heads) * wide, bytes_accessed=6 * 10**6, transcendentals=0
        ),
        name="out_project",
    )(*weights, *heads, *extra)


def local(n_ctx, n_tp, tokens, norm_gain, q_weight, k_weight, v_weight, o_weight, post_gain, doc_ids, plan):
    rows, features = tokens.shape
    blocks = rows // BLK
    total_blocks = doc_ids.shape[0]
    shard = lax.axis_index("ctx")
    cols = o_weight.shape[1] // n_tp

    def ctx_xor(a, m):
        return lax.ppermute(a, "ctx", [(i, i ^ m) for i in range(n_ctx)])

    def ctx_z(a, d):
        return lax.ppermute(a, "ctx", [(i, (i + d * PLANE) % n_ctx) for i in range(n_ctx)])

    def tp_xor(a, m):
        return lax.ppermute(a, "tp", [(i, i ^ m) for i in range(n_tp)])

    own_kv, *cuts = project(
        tokens, norm_gain, [k_weight, v_weight], None, "project_kv", o_weight, n_tp
    )
    (queries,) = project(tokens, norm_gain, [q_weight], query_scale, "project_q")

    first_block = jnp.sum((doc_ids[None, :] < doc_ids[:, None]).astype(jnp.int32), axis=1)
    own_first = lax.dynamic_slice_in_dim(first_block, shard * blocks, blocks, 0)
    plane_first = (shard // PLANE - BACK) * PLANE * blocks
    info = jnp.concatenate(
        [(shard % PLANE).reshape(1), (own_first - plane_first) * BLK]
    ).astype(jnp.int32)

    planes = [own_kv, ctx_z(own_kv, 1)]
    across = [ctx_xor(own_kv, 2)]
    cuts = [tp_xor(c, m) if m % 2 else c for m, c in enumerate(cuts)]
    planes, queries, cuts[2], plan = lax.optimization_barrier((planes, queries, cuts[2], plan))
    planes.append(ctx_z(planes[1], 1))
    across.append(ctx_xor(planes[1], 2))
    cuts[2] = tp_xor(cuts[2], 2)

    same = (plan[None, :] == plan[:, None]).astype(jnp.int32)
    block_ids = jnp.arange(total_blocks, dtype=jnp.int32)
    rank = jnp.sum(same * (block_ids[None, :] < block_ids[:, None]), axis=1)
    target = plan * blocks + rank
    picker = (target[None, :] == block_ids[:, None]).astype(jnp.bfloat16)

    carry = []
    for stage in range(BACK):
        near = planes[stage]
        kvs = [near, ctx_xor(near, 1), across[stage], ctx_xor(across[stage], 1)]
        carry = attend(stage, info, queries, kvs, carry)
        if stage == 0:
            planes[BACK], carry = lax.optimization_barrier((planes[BACK], carry))
            across.append(ctx_xor(planes[BACK], 2))
    mine = jnp.stack([c[0] for c in cuts])
    passed = jnp.stack([c[1] for c in cuts])
    far, carry, mine, passed, picker = lax.optimization_barrier(
        (across[BACK], carry, mine, passed, picker)
    )
    passed = tp_xor(passed, n_tp // 2)
    kvs = [planes[BACK], ctx_xor(planes[BACK], 1), far, ctx_xor(far, 1)]
    natural = attend(BACK, info, queries, kvs, carry)

    width = natural.shape[1]
    piece = BLK // n_ctx
    striped = natural.reshape(blocks, n_ctx, piece, width).transpose(1, 0, 2, 3)
    striped = striped.reshape(n_ctx, blocks, piece * width)
    gathered = lax.all_to_all(striped, "ctx", 0, 0, tiled=True)
    gathered, mine, passed = lax.optimization_barrier((gathered, mine, passed))
    weights = [mine, passed, ctx_xor(mine, 1), ctx_xor(passed, 1)]
    ordered = jnp.dot(
        picker,
        gathered.reshape(total_blocks, piece * width),
        preferred_element_type=jnp.float32,
    ).astype(jnp.bfloat16)
    placed = lax.all_to_all(
        ordered.reshape(n_ctx, blocks, piece * width), "ctx", 0, 0, tiled=True
    )
    placed = (
        placed.reshape(n_ctx, blocks, piece, width).transpose(1, 0, 2, 3).reshape(rows, width)
    )

    heads = [placed] + [None] * (n_tp - 1)
    for m in (4, 1, 3, 2):
        heads[m] = tp_xor(placed, m)
    heads[5] = tp_xor(heads[4], 1)
    heads[7] = tp_xor(heads[4], 3)
    heads[6] = tp_xor(heads[2], 4)
    half_tp = n_tp // 2
    near = tuple(range(half_tp))
    places = ((0, 0, near), (0, 0, (half_tp,)), (1, 0, near), (1, 0, (half_tp,)))
    (summed,) = out_project(heads[: half_tp + 1], weights, places)
    rest = tuple(range(half_tp - 1))
    places = ((0, 1, rest), (1, 1, rest))
    summed, squares = out_project(
        heads[half_tp + 1 :], weights[1::2], places, summed, cols
    )
    squares = squares.reshape(rows)
    squares = squares + tp_xor(squares, 4)
    squares = squares + tp_xor(squares, 2) + tp_xor(squares, 1) + tp_xor(squares, 3)
    scale = lax.rsqrt(squares / features + norm_eps)
    return (summed * scale[:, None] * post_gain).astype(jnp.bfloat16)


def solution(mesh):
    placed = (
        P("ctx", None),
        P(),
        P(None, "tp"),
        P(None, "tp"),
        P(None, "tp"),
        P("tp", None),
        P("tp"),
        P(),
        P(),
    )
    return jax.shard_map(
        functools.partial(local, mesh.shape["ctx"], mesh.shape["tp"]),
        mesh=mesh,
        in_specs=placed,
        out_specs=P("ctx", "tp"),
        check_vma=False,
    )
```

```python
import functools
import math

import jax
import jax.numpy as jnp
from jax import lax
from jax.experimental import pallas as pl
from jax.experimental.pallas import tpu as pltpu
from jax.sharding import PartitionSpec as P

HD = 128
BLK = 128
PLANE = 4
BACK = 2

query_scale = 144.0 ** (-0.5)
soft_cap = 50.0
norm_eps = 1e-06
LOG2E = math.log2(math.e)


def project_kernel(scale, tile, count, parts, x_hbm, g_ref, *refs):
    w_hbms, refs = refs[:count], refs[count:]
    o_hbm, refs = (refs[0], refs[1:]) if parts else (None, refs)
    out_ref, cut_refs, refs = refs[0], refs[1 : 1 + parts // 2], refs[1 + parts // 2 :]
    x_buf, normed_buf, w_buf, x_sems, w_sems, *cut_sems = refs
    tiles = x_buf.shape[0] // tile

    def span(i):
        return pl.ds(pl.multiple_of(i * tile, tile), tile)

    def x_copy(i):
        return pltpu.make_async_copy(x_hbm.at[span(i)], x_buf.at[span(i)], x_sems.at[i])

    width = w_buf.shape[1] // count
    w_copies = [
        pltpu.make_async_copy(
            w_hbms[j], w_buf.at[:, j * width : (j + 1) * width], w_sems.at[j]
        )
        for j in range(count)
    ]
    for i in range(tiles):
        x_copy(i).start()
    for copy in w_copies:
        copy.start()
    cuts = []
    if parts:
        core, group = lax.rem(lax.axis_index("ctx"), 2), lax.axis_index("tp")
        half, wide = cut_refs[0].shape[1:]
        cols = o_hbm.shape[1] // parts
        for m in range(parts):
            first = lax.div((group ^ m) * cols, HD) * HD
            cuts.append(
                pltpu.make_async_copy(
                    o_hbm.at[
                        pl.ds(pl.multiple_of(core * half, half), half),
                        pl.ds(pl.multiple_of(first, HD), wide),
                    ],
                    cut_refs[m % (parts // 2)].at[m // (parts // 2)],
                    cut_sems[0].at[m],
                )
            )
            cuts[-1].start()
    gain = g_ref[...].reshape(1, -1)
    depth = x_buf.shape[1]
    chunk = math.gcd(depth, 512)

    @pl.loop(0, tiles)
    def _(i):
        x_copy(i).wait()
        squares = None
        for at in range(0, depth, chunk):
            x = x_buf[span(i), at : at + chunk].astype(jnp.float32)
            squares = x * x if squares is None else squares + x * x
        r = lax.rsqrt(jnp.sum(squares, axis=1, keepdims=True) / depth + norm_eps)
        r = jnp.broadcast_to(r, (tile, chunk))
        for at in range(0, depth, chunk):
            x = x_buf[span(i), at : at + chunk].astype(jnp.float32)
            normed_buf[span(i), at : at + chunk] = (x * r * gain[:, at : at + chunk]).astype(
                jnp.bfloat16
            )

    for copy in w_copies:
        copy.wait()
    done = jnp.dot(normed_buf[...], w_buf[...], preferred_element_type=jnp.float32)
    if scale is not None:
        done = done * scale
    out_ref[...] = done.astype(jnp.bfloat16)
    for copy in cuts:
        copy.wait()


def project(tokens, gain, weights, scale, name, o_weight=None, parts=0):
    rows, d = tokens.shape
    tile = 64
    count = len(weights)
    width = sum(w.shape[1] for w in weights)
    anywhere = pl.BlockSpec(memory_space=pl.ANY)
    whole = pl.BlockSpec(memory_space=pltpu.VMEM)
    out_specs = [whole]
    out_shape = [jax.ShapeDtypeStruct((rows, width), jnp.bfloat16)]
    sems = [pltpu.SemaphoreType.DMA((rows // tile,)), pltpu.SemaphoreType.DMA((count,))]
    operands = [tokens, gain, *weights]
    if parts:
        wide = -(-(o_weight.shape[1] // parts) // HD) * HD
        out_specs += [whole] * (parts // 2)
        out_shape += [
            jax.ShapeDtypeStruct((2, o_weight.shape[0] // 2, wide), jnp.bfloat16)
        ] * (parts // 2)
        sems.append(pltpu.SemaphoreType.DMA((parts,)))
        operands.append(o_weight)
    return pl.pallas_call(
        functools.partial(project_kernel, scale, tile, count, parts),
        in_specs=[anywhere, whole] + [anywhere] * (len(operands) - 2),
        out_specs=out_specs,
        out_shape=out_shape,
        scratch_shapes=[
            pltpu.VMEM((rows, d), jnp.bfloat16),
            pltpu.VMEM((rows, d), jnp.bfloat16),
            pltpu.VMEM((d, width), jnp.bfloat16),
        ]
        + sems,
        compiler_params=pltpu.CompilerParams(vmem_limit_bytes=56 * 2**20),
        cost_estimate=pl.CostEstimate(
            flops=2 * rows * d * width, bytes_accessed=2 * d * (rows + width), transcendentals=0
        ),
        name=name,
    )(*operands)


def attend_kernel(rows, stage, info_ref, q_ref, *refs):
    kv_refs, refs = refs[:PLANE], refs[PLANE:]
    if stage == 0:
        num_ref, den_ref, held, sems = refs
    elif stage < BACK:
        num_in, den_in, num_ref, den_ref, held, sems = refs
    else:
        num_in, den_in, out_ref, num_ref, den_ref, held, sems = refs
    place = info_ref[0]
    copies = [
        pltpu.make_async_copy(kv_refs[i], held.at[place ^ i], sems.at[i]) for i in range(PLANE)
    ]
    for copy in copies:
        copy.start()
    if stage == 0:
        num_ref[...] = jnp.zeros_like(num_ref)
        den_ref[...] = jnp.zeros_like(den_ref)
    else:
        num_ref[...] = num_in[...]
        den_ref[...] = den_in[...]
    blocks = rows // BLK
    heads = num_ref.shape[0]
    base = (BACK - stage) * PLANE
    starts = [info_ref[1 + b] - base * rows for b in range(blocks)]
    row = lax.broadcasted_iota(jnp.int32, (rows, 1), 0)
    start_row = jnp.full((rows, 1), starts[0], jnp.int32)
    for b in range(1, blocks):
        start_row = jnp.where(row >= b * BLK, starts[b], start_row)

    def tile(s, lower, causal):
        for h in range(heads):
            scores = lax.dot_general(
                q_ref[:, h * HD : (h + 1) * HD],
                held[s, :, :HD],
                (((1,), (1,)), ((), ())),
                preferred_element_type=jnp.float32,
            )
            capped = jnp.tanh(scores * (1.0 / soft_cap)) * (soft_cap * LOG2E)
            weights = jnp.exp2(capped)
            if lower or causal:
                offset = lax.broadcasted_iota(jnp.int32, (rows, rows), 1)
                allowed = offset >= start_row - s * rows
                if causal:
                    allowed = allowed & (offset <= row)
                weights = jnp.where(allowed, weights, 0.0)
            weight_sum = weights[:, :HD]
            for j in range(1, rows // HD):
                weight_sum = weight_sum + weights[:, j * HD : (j + 1) * HD]
            den_ref[h] += weight_sum
            num_ref[h] += jnp.dot(
                weights.astype(jnp.bfloat16), held[s, :, HD:], preferred_element_type=jnp.float32
            )

    end = place if stage == 0 else PLANE
    lo = jnp.clip(lax.div(jnp.maximum(starts[0], 0), rows), 0, end)
    clear = jnp.clip(lax.div(jnp.maximum(starts[-1], 0) + rows - 1, rows), lo, end)
    for copy in copies:
        copy.wait()

    @pl.loop(lo, clear)
    def _(s):
        tile(s, True, False)

    @pl.loop(clear, end)
    def _(s):
        tile(s, False, False)

    if stage == 0:
        tile(place, True, True)
    if stage == BACK:
        for h in range(heads):
            total = jnp.sum(den_ref[h], axis=1, keepdims=True)
            out_ref[:, h * HD : (h + 1) * HD] = (num_ref[h] / total).astype(jnp.bfloat16)


def attend(stage, info, q, kvs, carry):
    rows = q.shape[0]
    heads = q.shape[1] // HD
    sums = jax.ShapeDtypeStruct((heads, rows, HD), jnp.float32)
    last = stage == BACK
    whole = pl.BlockSpec(memory_space=pltpu.VMEM)
    return pl.pallas_call(
        functools.partial(attend_kernel, rows, stage),
        in_specs=[pl.BlockSpec(memory_space=pltpu.SMEM), whole]
        + [pl.BlockSpec(memory_space=pl.ANY)] * PLANE
        + [whole] * len(carry),
        out_specs=whole if last else [whole] * 2,
        out_shape=jax.ShapeDtypeStruct(q.shape, jnp.bfloat16) if last else [sums] * 2,
        scratch_shapes=([pltpu.VMEM(sums.shape, jnp.float32)] * 2 if last else [])
        + [
            pltpu.VMEM((PLANE, rows, 2 * HD), jnp.bfloat16),
            pltpu.SemaphoreType.DMA((PLANE,)),
        ],
        compiler_params=pltpu.CompilerParams(vmem_limit_bytes=32 * 2**20),
        cost_estimate=pl.CostEstimate(
            flops=2 * 10**9, bytes_accessed=4 * 10**6, transcendentals=4 * 10**6
        ),
        name="attend",
    )(info, q, *kvs, *carry)


def out_kernel(heads, cols, places, *refs):
    count = len(places)
    w_refs, refs = refs[:count], refs[count:]
    head_refs, refs = refs[:heads], refs[heads:]
    total = None
    if cols:
        before_ref, sum_ref, square_ref, lhs = refs
        total = before_ref[...]
    else:
        sum_ref, lhs = refs
    core, group = lax.rem(lax.axis_index("ctx"), 2), lax.axis_index("tp")
    half, wide = w_refs[0].shape[1:]
    at = 0
    for w_ref, (side, first_group, members) in zip(w_refs, places):
        side = core if side == 0 else 1 - core
        span = pl.ds(pl.multiple_of(side * half, half), half)
        first = at
        for m in members:
            lhs[:, at : at + half] = head_refs[m][:, span]
            at += half
        product = jnp.dot(
            lhs[:, first:at],
            w_ref[first_group : first_group + len(members)].reshape(at - first, wide),
            preferred_element_type=jnp.float32,
        )
        total = product if total is None else total + product
    if not cols:
        sum_ref[...] = total
        return
    total = jnp.where(group % 2 == 1, total[:, wide - cols :], total[:, :cols])
    sum_ref[...] = total
    square = total * total
    high = square.astype(jnp.bfloat16)
    low = (square - high.astype(jnp.float32)).astype(jnp.bfloat16)
    ones = jnp.ones((16, cols), jnp.bfloat16)
    sums = None
    for part in (high, low):
        product = lax.dot_general(
            ones, part, (((1,), (1,)), ((), ())), preferred_element_type=jnp.float32
        )
        sums = product if sums is None else sums + product
    square_ref[...] = sums[:1]


def out_project(heads, weights, places, before=None, cols=0):
    rows, inner = heads[0].shape
    wide = weights[0].shape[2]
    whole = pl.BlockSpec(memory_space=pltpu.VMEM)
    if cols:
        out_shape = [
            jax.ShapeDtypeStruct((rows, cols), jnp.float32),
            jax.ShapeDtypeStruct((1, rows), jnp.float32),
        ]
        extra = [before]
    else:
        out_shape = [jax.ShapeDtypeStruct((rows, wide), jnp.float32)]
        extra = []
    return pl.pallas_call(
        functools.partial(out_kernel, len(heads), cols, places),
        in_specs=[whole] * (len(heads) + len(weights) + len(extra)),
        out_specs=[whole] * len(out_shape),
        out_shape=out_shape,
        scratch_shapes=[pltpu.VMEM((rows, len(heads) * inner), jnp.bfloat16)],
        compiler_params=pltpu.CompilerParams(vmem_limit_bytes=32 * 2**20),
        cost_estimate=pl.CostEstimate(
            flops=2 * rows * inner * len(heads) * wide, bytes_accessed=6 * 10**6, transcendentals=0
        ),
        name="out_project",
    )(*weights, *heads, *extra)


def local(n_ctx, n_tp, tokens, norm_gain, q_weight, k_weight, v_weight, o_weight, post_gain, doc_ids, plan):
    rows, features = tokens.shape
    blocks = rows // BLK
    total_blocks = doc_ids.shape[0]
    shard = lax.axis_index("ctx")
    cols = o_weight.shape[1] // n_tp

    def ctx_xor(a, m):
        return lax.ppermute(a, "ctx", [(i, i ^ m) for i in range(n_ctx)])

    def ctx_z(a, d):
        return lax.ppermute(a, "ctx", [(i, (i + d * PLANE) % n_ctx) for i in range(n_ctx)])

    def tp_xor(a, m):
        return lax.ppermute(a, "tp", [(i, i ^ m) for i in range(n_tp)])

    own_kv, *cuts = project(
        tokens, norm_gain, [k_weight, v_weight], None, "project_kv", o_weight, n_tp
    )
    (queries,) = project(tokens, norm_gain, [q_weight], query_scale, "project_q")

    first_block = jnp.sum((doc_ids[None, :] < doc_ids[:, None]).astype(jnp.int32), axis=1)
    own_first = lax.dynamic_slice_in_dim(first_block, shard * blocks, blocks, 0)
    plane_first = (shard // PLANE - BACK) * PLANE * blocks
    info = jnp.concatenate(
        [(shard % PLANE).reshape(1), (own_first - plane_first) * BLK]
    ).astype(jnp.int32)

    planes = [own_kv, ctx_z(own_kv, 1)]
    across = [ctx_xor(own_kv, 2)]
    cuts = [tp_xor(c, m) if m % 2 else c for m, c in enumerate(cuts)]
    planes, queries, cuts[2], plan = lax.optimization_barrier((planes, queries, cuts[2], plan))
    planes.append(ctx_z(planes[1], 1))
    across.append(ctx_xor(planes[1], 2))
    cuts[2] = tp_xor(cuts[2], 2)

    same = (plan[None, :] == plan[:, None]).astype(jnp.int32)
    block_ids = jnp.arange(total_blocks, dtype=jnp.int32)
    rank = jnp.sum(same * (block_ids[None, :] < block_ids[:, None]), axis=1)
    target = plan * blocks + rank
    lines = BLK // n_ctx // 2
    line_ids = jnp.arange(total_blocks * lines, dtype=jnp.int32)
    line_target = (target[:, None] * lines + jnp.arange(lines, dtype=jnp.int32)).reshape(-1)
    picker = (line_target[None, :] == line_ids[:, None]).astype(jnp.bfloat16)

    carry = []
    for stage in range(BACK):
        near = planes[stage]
        kvs = [near, ctx_xor(near, 1), across[stage], ctx_xor(across[stage], 1)]
        carry = attend(stage, info, queries, kvs, carry)
        if stage == 0:
            planes[BACK], carry = lax.optimization_barrier((planes[BACK], carry))
            across.append(ctx_xor(planes[BACK], 2))
    mine = jnp.stack([c[0] for c in cuts])
    passed = jnp.stack([c[1] for c in cuts])
    far, carry, mine, passed, picker = lax.optimization_barrier(
        (across[BACK], carry, mine, passed, picker)
    )
    passed = tp_xor(passed, n_tp // 2)
    kvs = [planes[BACK], ctx_xor(planes[BACK], 1), far, ctx_xor(far, 1)]
    natural = attend(BACK, info, queries, kvs, carry)

    width = natural.shape[1]
    piece, fold = BLK // n_ctx, 2
    striped = natural.reshape(blocks, n_ctx, piece, width).transpose(1, 0, 2, 3)
    striped = striped.reshape(n_ctx, blocks * piece // fold, fold * width)
    gathered = lax.all_to_all(striped, "ctx", 0, 0, tiled=True)
    gathered, mine, passed = lax.optimization_barrier((gathered, mine, passed))
    weights = [mine, passed, ctx_xor(mine, 1), ctx_xor(passed, 1)]
    ordered = jnp.dot(
        picker,
        gathered.reshape(total_blocks * piece // fold, fold * width),
        preferred_element_type=jnp.float32,
    ).astype(jnp.bfloat16)
    placed = lax.all_to_all(ordered.reshape(striped.shape), "ctx", 0, 0, tiled=True)
    placed, weights = lax.optimization_barrier((placed, weights))
    placed = (
        placed.reshape(n_ctx, blocks, piece, width).transpose(1, 0, 2, 3).reshape(rows, width)
    )

    heads = [placed] + [None] * (n_tp - 1)
    for m in (4, 1, 3, 2):
        heads[m] = tp_xor(placed, m)
    heads[5] = tp_xor(heads[4], 1)
    heads[7] = tp_xor(heads[4], 3)
    heads[6] = tp_xor(heads[2], 4)
    half_tp = n_tp // 2
    near = tuple(range(half_tp))
    places = ((0, 0, near), (0, 0, (half_tp,)), (1, 0, near), (1, 0, (half_tp,)))
    (summed,) = out_project(heads[: half_tp + 1], weights, places)
    rest = tuple(range(half_tp - 1))
    places = ((0, 1, rest), (1, 1, rest))
    summed, squares = out_project(
        heads[half_tp + 1 :], weights[1::2], places, summed, cols
    )
    squares = squares.reshape(rows)
    squares = squares + tp_xor(squares, 4)
    squares = squares + tp_xor(squares, 2) + tp_xor(squares, 1) + tp_xor(squares, 3)
    scale = lax.rsqrt(squares / features + norm_eps)
    return (summed * scale[:, None] * post_gain).astype(jnp.bfloat16)


def solution(mesh):
    placed = (
        P("ctx", None),
        P(),
        P(None, "tp"),
        P(None, "tp"),
        P(None, "tp"),
        P("tp", None),
        P("tp"),
        P(),
        P(),
    )
    return jax.shard_map(
        functools.partial(local, mesh.shape["ctx"], mesh.shape["tp"]),
        mesh=mesh,
        in_specs=placed,
        out_specs=P("ctx", "tp"),
        check_vma=False,
    )
```

```python
import functools
import math

import jax
import jax.numpy as jnp
from jax import lax
from jax.experimental import pallas as pl
from jax.experimental.pallas import tpu as pltpu
from jax.sharding import PartitionSpec as P

HD = 128
BLK = 128
PLANE = 4
BACK = 2

query_scale = 144.0 ** (-0.5)
soft_cap = 50.0
norm_eps = 1e-06
LOG2E = math.log2(math.e)


def project_kernel(scale, tile, count, parts, x_hbm, g_ref, *refs):
    w_hbms, refs = refs[:count], refs[count:]
    o_hbm, refs = (refs[0], refs[1:]) if parts else (None, refs)
    out_ref, cut_refs, refs = refs[0], refs[1 : 1 + parts // 2], refs[1 + parts // 2 :]
    x_buf, normed_buf, w_buf, x_sems, w_sems, *cut_sems = refs
    tiles = x_buf.shape[0] // tile

    def span(i):
        return pl.ds(pl.multiple_of(i * tile, tile), tile)

    def x_copy(i):
        return pltpu.make_async_copy(x_hbm.at[span(i)], x_buf.at[span(i)], x_sems.at[i])

    width = w_buf.shape[1] // count
    w_copies = [
        pltpu.make_async_copy(
            w_hbms[j], w_buf.at[:, j * width : (j + 1) * width], w_sems.at[j]
        )
        for j in range(count)
    ]
    for i in range(tiles):
        x_copy(i).start()
    for copy in w_copies:
        copy.start()
    cuts = []
    if parts:
        core, group = lax.rem(lax.axis_index("ctx"), 2), lax.axis_index("tp")
        half, wide = cut_refs[0].shape[1:]
        cols = o_hbm.shape[1] // parts
        for m in range(parts):
            first = lax.div((group ^ m) * cols, HD) * HD
            cuts.append(
                pltpu.make_async_copy(
                    o_hbm.at[
                        pl.ds(pl.multiple_of(core * half, half), half),
                        pl.ds(pl.multiple_of(first, HD), wide),
                    ],
                    cut_refs[m % (parts // 2)].at[m // (parts // 2)],
                    cut_sems[0].at[m],
                )
            )
            cuts[-1].start()
    gain = g_ref[...].reshape(1, -1)
    depth = x_buf.shape[1]
    chunk = math.gcd(depth, 512)

    @pl.loop(0, tiles)
    def _(i):
        x_copy(i).wait()
        squares = None
        for at in range(0, depth, chunk):
            x = x_buf[span(i), at : at + chunk].astype(jnp.float32)
            squares = x * x if squares is None else squares + x * x
        r = lax.rsqrt(jnp.sum(squares, axis=1, keepdims=True) / depth + norm_eps)
        r = jnp.broadcast_to(r, (tile, chunk))
        for at in range(0, depth, chunk):
            x = x_buf[span(i), at : at + chunk].astype(jnp.float32)
            normed_buf[span(i), at : at + chunk] = (x * r * gain[:, at : at + chunk]).astype(
                jnp.bfloat16
            )

    for copy in w_copies:
        copy.wait()
    done = jnp.dot(normed_buf[...], w_buf[...], preferred_element_type=jnp.float32)
    if scale is not None:
        done = done * scale
    out_ref[...] = done.astype(jnp.bfloat16)
    for copy in cuts:
        copy.wait()


def project(tokens, gain, weights, scale, name, o_weight=None, parts=0):
    rows, d = tokens.shape
    tile = 64
    count = len(weights)
    width = sum(w.shape[1] for w in weights)
    anywhere = pl.BlockSpec(memory_space=pl.ANY)
    whole = pl.BlockSpec(memory_space=pltpu.VMEM)
    out_specs = [whole]
    out_shape = [jax.ShapeDtypeStruct((rows, width), jnp.bfloat16)]
    sems = [pltpu.SemaphoreType.DMA((rows // tile,)), pltpu.SemaphoreType.DMA((count,))]
    operands = [tokens, gain, *weights]
    if parts:
        wide = -(-(o_weight.shape[1] // parts) // HD) * HD
        out_specs += [whole] * (parts // 2)
        out_shape += [
            jax.ShapeDtypeStruct((2, o_weight.shape[0] // 2, wide), jnp.bfloat16)
        ] * (parts // 2)
        sems.append(pltpu.SemaphoreType.DMA((parts,)))
        operands.append(o_weight)
    return pl.pallas_call(
        functools.partial(project_kernel, scale, tile, count, parts),
        in_specs=[anywhere, whole] + [anywhere] * (len(operands) - 2),
        out_specs=out_specs,
        out_shape=out_shape,
        scratch_shapes=[
            pltpu.VMEM((rows, d), jnp.bfloat16),
            pltpu.VMEM((rows, d), jnp.bfloat16),
            pltpu.VMEM((d, width), jnp.bfloat16),
        ]
        + sems,
        compiler_params=pltpu.CompilerParams(vmem_limit_bytes=56 * 2**20),
        cost_estimate=pl.CostEstimate(
            flops=2 * rows * d * width, bytes_accessed=2 * d * (rows + width), transcendentals=0
        ),
        name=name,
    )(*operands)


def attend_kernel(rows, stage, info_ref, q_ref, *refs):
    kv_refs, refs = refs[:PLANE], refs[PLANE:]
    if stage == 0:
        num_ref, den_ref, held, sems = refs
    elif stage < BACK:
        num_in, den_in, num_ref, den_ref, held, sems = refs
    else:
        num_in, den_in, out_ref, num_ref, den_ref, held, sems = refs
    place = info_ref[0]
    copies = [
        pltpu.make_async_copy(kv_refs[i], held.at[place ^ i], sems.at[i]) for i in range(PLANE)
    ]
    for copy in copies:
        copy.start()
    if stage == 0:
        num_ref[...] = jnp.zeros_like(num_ref)
        den_ref[...] = jnp.zeros_like(den_ref)
    else:
        num_ref[...] = num_in[...]
        den_ref[...] = den_in[...]
    blocks = rows // BLK
    heads = num_ref.shape[0]
    base = (BACK - stage) * PLANE
    starts = [info_ref[1 + b] - base * rows for b in range(blocks)]
    row = lax.broadcasted_iota(jnp.int32, (rows, 1), 0)
    start_row = jnp.full((rows, 1), starts[0], jnp.int32)
    for b in range(1, blocks):
        start_row = jnp.where(row >= b * BLK, starts[b], start_row)

    def tile(s, lower, causal):
        for h in range(heads):
            scores = lax.dot_general(
                q_ref[:, h * HD : (h + 1) * HD],
                held[s, :, :HD],
                (((1,), (1,)), ((), ())),
                preferred_element_type=jnp.float32,
            )
            capped = jnp.tanh(scores * (1.0 / soft_cap)) * (soft_cap * LOG2E)
            weights = jnp.exp2(capped)
            if lower or causal:
                offset = lax.broadcasted_iota(jnp.int32, (rows, rows), 1)
                allowed = offset >= start_row - s * rows
                if causal:
                    allowed = allowed & (offset <= row)
                weights = jnp.where(allowed, weights, 0.0)
            weight_sum = weights[:, :HD]
            for j in range(1, rows // HD):
                weight_sum = weight_sum + weights[:, j * HD : (j + 1) * HD]
            den_ref[h] += weight_sum
            num_ref[h] += jnp.dot(
                weights.astype(jnp.bfloat16), held[s, :, HD:], preferred_element_type=jnp.float32
            )

    end = place if stage == 0 else PLANE
    lo = jnp.clip(lax.div(jnp.maximum(starts[0], 0), rows), 0, end)
    clear = jnp.clip(lax.div(jnp.maximum(starts[-1], 0) + rows - 1, rows), lo, end)
    copies[0].wait()
    if stage == 0:
        tile(place, True, True)
    for copy in copies[1:]:
        copy.wait()

    @pl.loop(lo, clear)
    def _(s):
        tile(s, True, False)

    @pl.loop(clear, end)
    def _(s):
        tile(s, False, False)

    if stage == BACK:
        for h in range(heads):
            total = jnp.sum(den_ref[h], axis=1, keepdims=True)
            out_ref[:, h * HD : (h + 1) * HD] = (num_ref[h] / total).astype(jnp.bfloat16)


def attend(stage, info, q, kvs, carry):
    rows = q.shape[0]
    heads = q.shape[1] // HD
    sums = jax.ShapeDtypeStruct((heads, rows, HD), jnp.float32)
    last = stage == BACK
    whole = pl.BlockSpec(memory_space=pltpu.VMEM)
    return pl.pallas_call(
        functools.partial(attend_kernel, rows, stage),
        in_specs=[pl.BlockSpec(memory_space=pltpu.SMEM), whole]
        + [pl.BlockSpec(memory_space=pl.ANY)] * PLANE
        + [whole] * len(carry),
        out_specs=whole if last else [whole] * 2,
        out_shape=jax.ShapeDtypeStruct(q.shape, jnp.bfloat16) if last else [sums] * 2,
        scratch_shapes=([pltpu.VMEM(sums.shape, jnp.float32)] * 2 if last else [])
        + [
            pltpu.VMEM((PLANE, rows, 2 * HD), jnp.bfloat16),
            pltpu.SemaphoreType.DMA((PLANE,)),
        ],
        compiler_params=pltpu.CompilerParams(vmem_limit_bytes=32 * 2**20),
        cost_estimate=pl.CostEstimate(
            flops=2 * 10**9, bytes_accessed=4 * 10**6, transcendentals=4 * 10**6
        ),
        name="attend",
    )(info, q, *kvs, *carry)


def out_kernel(heads, cols, places, *refs):
    count = len(places)
    w_refs, refs = refs[:count], refs[count:]
    head_refs, refs = refs[:heads], refs[heads:]
    total = None
    if cols:
        before_ref, sum_ref, square_ref, lhs = refs
        total = before_ref[...]
    else:
        sum_ref, lhs = refs
    core, group = lax.rem(lax.axis_index("ctx"), 2), lax.axis_index("tp")
    half, wide = w_refs[0].shape[1:]
    at = 0
    for w_ref, (side, first_group, members) in zip(w_refs, places):
        side = core if side == 0 else 1 - core
        span = pl.ds(pl.multiple_of(side * half, half), half)
        first = at
        for m in members:
            lhs[:, at : at + half] = head_refs[m][:, span]
            at += half
        product = jnp.dot(
            lhs[:, first:at],
            w_ref[first_group : first_group + len(members)].reshape(at - first, wide),
            preferred_element_type=jnp.float32,
        )
        total = product if total is None else total + product
    if not cols:
        sum_ref[...] = total
        return
    total = jnp.where(group % 2 == 1, total[:, wide - cols :], total[:, :cols])
    sum_ref[...] = total
    square = total * total
    high = square.astype(jnp.bfloat16)
    low = (square - high.astype(jnp.float32)).astype(jnp.bfloat16)
    ones = jnp.ones((16, cols), jnp.bfloat16)
    sums = None
    for part in (high, low):
        product = lax.dot_general(
            ones, part, (((1,), (1,)), ((), ())), preferred_element_type=jnp.float32
        )
        sums = product if sums is None else sums + product
    square_ref[...] = sums[:1]


def out_project(heads, weights, places, before=None, cols=0):
    rows, inner = heads[0].shape
    wide = weights[0].shape[2]
    whole = pl.BlockSpec(memory_space=pltpu.VMEM)
    if cols:
        out_shape = [
            jax.ShapeDtypeStruct((rows, cols), jnp.float32),
            jax.ShapeDtypeStruct((1, rows), jnp.float32),
        ]
        extra = [before]
    else:
        out_shape = [jax.ShapeDtypeStruct((rows, wide), jnp.float32)]
        extra = []
    return pl.pallas_call(
        functools.partial(out_kernel, len(heads), cols, places),
        in_specs=[whole] * (len(heads) + len(weights) + len(extra)),
        out_specs=[whole] * len(out_shape),
        out_shape=out_shape,
        scratch_shapes=[pltpu.VMEM((rows, len(heads) * inner), jnp.bfloat16)],
        compiler_params=pltpu.CompilerParams(vmem_limit_bytes=32 * 2**20),
        cost_estimate=pl.CostEstimate(
            flops=2 * rows * inner * len(heads) * wide, bytes_accessed=6 * 10**6, transcendentals=0
        ),
        name="out_project",
    )(*weights, *heads, *extra)


def local(n_ctx, n_tp, tokens, norm_gain, q_weight, k_weight, v_weight, o_weight, post_gain, doc_ids, plan):
    rows, features = tokens.shape
    blocks = rows // BLK
    total_blocks = doc_ids.shape[0]
    shard = lax.axis_index("ctx")
    cols = o_weight.shape[1] // n_tp

    def ctx_xor(a, m):
        return lax.ppermute(a, "ctx", [(i, i ^ m) for i in range(n_ctx)])

    def ctx_z(a, d):
        return lax.ppermute(a, "ctx", [(i, (i + d * PLANE) % n_ctx) for i in range(n_ctx)])

    def tp_xor(a, m):
        return lax.ppermute(a, "tp", [(i, i ^ m) for i in range(n_tp)])

    own_kv, *cuts = project(
        tokens, norm_gain, [k_weight, v_weight], None, "project_kv", o_weight, n_tp
    )
    (queries,) = project(tokens, norm_gain, [q_weight], query_scale, "project_q")

    first_block = jnp.sum((doc_ids[None, :] < doc_ids[:, None]).astype(jnp.int32), axis=1)
    own_first = lax.dynamic_slice_in_dim(first_block, shard * blocks, blocks, 0)
    plane_first = (shard // PLANE - BACK) * PLANE * blocks
    info = jnp.concatenate(
        [(shard % PLANE).reshape(1), (own_first - plane_first) * BLK]
    ).astype(jnp.int32)

    planes = [own_kv, ctx_z(own_kv, 1)]
    across = [ctx_xor(own_kv, 2)]
    cuts = [tp_xor(c, m) if m % 2 else c for m, c in enumerate(cuts)]
    planes, queries, cuts[2], plan = lax.optimization_barrier((planes, queries, cuts[2], plan))
    planes.append(ctx_z(planes[1], 1))
    across.append(ctx_xor(planes[1], 2))
    cuts[2] = tp_xor(cuts[2], 2)

    same = (plan[None, :] == plan[:, None]).astype(jnp.int32)
    block_ids = jnp.arange(total_blocks, dtype=jnp.int32)
    rank = jnp.sum(same * (block_ids[None, :] < block_ids[:, None]), axis=1)
    target = plan * blocks + rank
    lines = BLK // n_ctx // 2
    line_ids = jnp.arange(total_blocks * lines, dtype=jnp.int32)
    line_target = (target[:, None] * lines + jnp.arange(lines, dtype=jnp.int32)).reshape(-1)
    picker = (line_target[None, :] == line_ids[:, None]).astype(jnp.bfloat16)

    carry = []
    for stage in range(BACK):
        near = planes[stage]
        kvs = [near, ctx_xor(near, 1), across[stage], ctx_xor(across[stage], 1)]
        carry = attend(stage, info, queries, kvs, carry)
        if stage == 0:
            planes[BACK], carry = lax.optimization_barrier((planes[BACK], carry))
            across.append(ctx_xor(planes[BACK], 2))
    mine = jnp.stack([c[0] for c in cuts])
    passed = jnp.stack([c[1] for c in cuts])
    far, carry, mine, passed, picker = lax.optimization_barrier(
        (across[BACK], carry, mine, passed, picker)
    )
    passed = tp_xor(passed, n_tp // 2)
    kvs = [planes[BACK], ctx_xor(planes[BACK], 1), far, ctx_xor(far, 1)]
    natural = attend(BACK, info, queries, kvs, carry)

    width = natural.shape[1]
    piece, fold = BLK // n_ctx, 2
    striped = natural.reshape(blocks, n_ctx, piece, width).transpose(1, 0, 2, 3)
    striped = striped.reshape(n_ctx, blocks * piece // fold, fold * width)
    gathered = lax.all_to_all(striped, "ctx", 0, 0, tiled=True)
    gathered, mine, passed = lax.optimization_barrier((gathered, mine, passed))
    weights = [mine, passed, ctx_xor(mine, 1), ctx_xor(passed, 1)]
    ordered = jnp.dot(
        picker,
        gathered.reshape(total_blocks * piece // fold, fold * width),
        preferred_element_type=jnp.float32,
    ).astype(jnp.bfloat16)
    placed = lax.all_to_all(ordered.reshape(striped.shape), "ctx", 0, 0, tiled=True)
    placed, weights = lax.optimization_barrier((placed, weights))
    placed = (
        placed.reshape(n_ctx, blocks, piece, width).transpose(1, 0, 2, 3).reshape(rows, width)
    )

    heads = [placed] + [None] * (n_tp - 1)
    for m in (4, 1, 3, 2):
        heads[m] = tp_xor(placed, m)
    heads[5] = tp_xor(heads[4], 1)
    heads[7] = tp_xor(heads[4], 3)
    heads[6] = tp_xor(heads[2], 4)
    half_tp = n_tp // 2
    near = tuple(range(half_tp))
    places = ((0, 0, near), (0, 0, (half_tp,)), (1, 0, near), (1, 0, (half_tp,)))
    (summed,) = out_project(heads[: half_tp + 1], weights, places)
    rest = tuple(range(half_tp - 1))
    places = ((0, 1, rest), (1, 1, rest))
    summed, squares = out_project(
        heads[half_tp + 1 :], weights[1::2], places, summed, cols
    )
    squares = squares.reshape(rows)
    squares = squares + tp_xor(squares, 4)
    squares = squares + tp_xor(squares, 2) + tp_xor(squares, 1) + tp_xor(squares, 3)
    scale = lax.rsqrt(squares / features + norm_eps)
    return (summed * scale[:, None] * post_gain).astype(jnp.bfloat16)


def solution(mesh):
    placed = (
        P("ctx", None),
        P(),
        P(None, "tp"),
        P(None, "tp"),
        P(None, "tp"),
        P("tp", None),
        P("tp"),
        P(),
        P(),
    )
    return jax.shard_map(
        functools.partial(local, mesh.shape["ctx"], mesh.shape["tp"]),
        mesh=mesh,
        in_specs=placed,
        out_specs=P("ctx", "tp"),
        check_vma=False,
    )
```
